32 devices in a mesh: row: 8 (over y, x, core), col: 4 (over z).
Axes of the slice: x: 2, y: 2, z: 4, core: 2. Of those that a mesh axis runs over, the one named last changes fastest.
Arguments:
- orbitals: bfloat16 [32768, 512], P(('row', 'col')), may hold values from -6 to 6
- coulomb: bfloat16 [8192, 8192], P('row', 'col'), may hold values from -0.0029296875 to 0.0029296875
- interp: bfloat16 [32768, 1024], P(('row', 'col')), may hold values from -0.1875 to 0.1875
- box_counts: int32 [32], replicated, may hold values from 1 to 768, 8192 in all
- owner_map: int32 [8192], replicated, may hold values from 0 to 8191, as said below
- grid_rows: int32 [32, 1024], P(('row', 'col')), may hold values from 0 to 1023, each once within a row
- listed: int32 [32, 1024], P(('row', 'col')), may hold values from 0 to 255
Outputs:
- exchange_action: float32 [32768, 512], P(('row', 'col'))
The draws below stay inside these ranges and needn't reach their ends.
Inputs may be any that keep to these rules, and one draw needn't show every extreme that they name: `box_counts`: the counts sum to 8192; the largest is exactly 768. `owner_map`: A permutation of the 8192 positions; a point's owner is position // 256. No box holds more than 24 points of one owner, and the box with 768 points holds exactly 24 of some owner. `grid_rows`: each row is a permutation.
All inputs are finite; a program needn't handle non-finite values.
Results may differ from the reference program's by a relative error of at most 0.012.
Values may be sent and summed in bfloat16 or wider, within the bound.
No kernel may reach another device: no remote copies, remote signals or barrier semaphores. Data moves between devices by JAX's collectives and lax.ppermute only.
A program may use at most 128 MiB of HBM per device.

```python
import math
import jax
import jax.numpy as jnp
import numpy as np
from jax import lax

NORB = 512
LIST = 1024
OWN = 256
BOX = 1024
BOXES = 32
NMU = 8192
SLOTS = 768
PER = 32
TILE_R = 1024
N_ROW = 8
N_COL = 4


def draw_owner_map(key, part):
    first_key, second_key = jax.random.split(key)
    owner_order = jax.random.permutation(first_key, BOXES)
    local_order = jax.vmap(lambda subkey: jax.random.permutation(subkey, OWN))(jax.random.split(second_key, BOXES))
    listing = jnp.arange(OWN * BOXES)
    owner_ids = owner_order[listing % BOXES]
    local_ids = local_order[owner_ids, listing // BOXES]
    return (owner_ids * OWN + local_ids).astype(jnp.int32)


def plant(array, own_key, low, high):
    shape = array.shape
    spot = [jax.random.randint(jax.random.fold_in(own_key, axis), (), 0, shape[axis]) for axis in range(len(shape))]
    array = array.at[tuple(spot)].set(low)
    longest = shape.index(max(shape))
    spot[longest] = (spot[longest] + 1) % shape[longest]
    return array.at[tuple(spot)].set(high)


def steps_of(rng, dims, cuts, smallest, top_value):
    def one(dim, parts):
        steps = jax.random.uniform(jax.random.fold_in(jax.random.fold_in(rng, 6), dim), (parts,), jnp.float32, smallest / len(cuts), top_value / len(cuts))
        return jnp.repeat(jnp.exp(steps), dims[dim] // parts).reshape((-1,) + (1,) * (len(dims) - dim - 1))

    gain = one(*cuts[0])
    for cut in cuts[1:]:
        gain = gain * one(*cut)
    return gain


def length_profile(amount, total, reach, skew):
    loads = [(1 << 20) // math.isqrt(standing ** skew) + 1 for standing in range(2, amount + 1)]
    surplus, holding = total - reach - (amount - 1), [1] * (amount - 1)
    while surplus > 0:
        free = [i for i in range(amount - 1) if holding[i] < reach]
        mass, budget = sum([loads[i] for i in free]), surplus
        for i in free:
            addition = min(reach - holding[i], max(1, budget * loads[i] // mass), surplus)
            holding[i] = holding[i] + addition
            surplus = surplus - addition
    return np.array([reach] + holding)


def ragged(key, count, total, bound, slope):
    if count == 2:
        one = jax.random.randint(key, (), max(1, total - bound), min(bound, total - 1) + 1)
        return jnp.stack([one, total - one])
    sizes = jnp.asarray(length_profile(count, total, bound, slope), jnp.int32)
    couples = (count - 1) // 2
    donor, sink = sizes[1:1 + 2 * couples:2], sizes[2:2 + 2 * couples:2]
    margin = jnp.minimum(donor - 1, bound - sink)
    moved = jax.random.randint(jax.random.fold_in(key, 1), (couples,), 0, 1 << 20) % (margin + 1)
    sizes = sizes.at[1:1 + 2 * couples:2].set(donor - moved).at[2:2 + 2 * couples:2].set(sink + moved)
    return sizes[jax.random.permutation(jax.random.fold_in(key, 2), count)]


def scatter_about(key, extent, spread, bound, cuts=(), kind=jnp.bfloat16):
    drawn = jax.random.normal(key, extent, jnp.float32) * spread
    if len(cuts) > 0:
        drawn = steps_of(key, extent, cuts, -0.22, 0.18) * drawn
    return jnp.clip(drawn, min=-bound, max=bound).astype(kind)


def setup_inputs(seed: int = 0) -> dict:
    streams_of = jax.random.split(jax.random.key(seed), 8)
    orbitals = scatter_about(streams_of[0], (BOXES * BOX, NORB), 1.0, 6.0, ((0, 32),))
    coulomb = scatter_about(streams_of[1], (NMU, NMU), (NMU * NORB) ** -0.5, 0.0029296875, ((0, 8), (1, 4)))
    interp = scatter_about(streams_of[2], (BOXES * BOX, LIST), LIST ** -0.5, 0.1875, ((0, 32),))
    box_counts = ragged(streams_of[3], BOXES, NMU, SLOTS, 2).astype(jnp.int32)
    owner_map = draw_owner_map(jax.random.fold_in(streams_of[7], 71), 0)
    grid_rows = jax.vmap(lambda own: jax.random.permutation(own, BOX))(jax.random.split(streams_of[5], BOXES)).reshape((BOXES, BOX)).astype(jnp.int32)
    listed = plant(jax.random.randint(streams_of[6], (BOXES, LIST), 0, OWN), jax.random.fold_in(streams_of[6], 1), 0, OWN - 1).astype(jnp.int32)
    return {"orbitals": orbitals, "coulomb": coulomb, "interp": interp, "box_counts": box_counts, "owner_map": owner_map, "grid_rows": grid_rows, "listed": listed}


def reference(orbitals, coulomb, interp, box_counts, owner_map, grid_rows, listed):
    box_total = N_ROW * N_COL
    point_total = OWN * box_total
    box_ends = jnp.cumsum(box_counts).astype(jnp.int32)
    starts = (box_ends - box_counts).astype(jnp.int32)
    listing = jnp.arange(point_total, dtype=jnp.int32)
    source = jnp.sum((listing[:, None] >= box_ends[None, :]).astype(jnp.int32), axis=1).astype(jnp.int32)
    within = (listing - starts[source]).astype(jnp.int32)
    grid_index = (source * BOX + grid_rows[source, within]).astype(jnp.int32)
    point_rows = jnp.zeros((point_total, NORB), jnp.bfloat16).at[owner_map].set(orbitals[grid_index])
    column_rows = point_rows.reshape(N_ROW, N_COL, OWN, NORB).transpose(1, 0, 2, 3).reshape(point_total, NORB)
    right_rows = column_rows.astype(jnp.float32)

    def row_block(pieces):
        left_rows, kernel_rows = pieces
        pair_tile = jnp.dot(left_rows.astype(jnp.float32), right_rows.T, precision=lax.Precision.HIGHEST).astype(jnp.bfloat16)
        weighted = (pair_tile.astype(jnp.float32) * kernel_rows.astype(jnp.float32)).astype(jnp.bfloat16)
        return jnp.dot(weighted.astype(jnp.float32), right_rows, precision=lax.Precision.HIGHEST)

    projected = lax.map(row_block, (point_rows.reshape(N_ROW, TILE_R, NORB), coulomb.reshape(N_ROW, TILE_R, point_total)))
    projected = projected.reshape(point_total, NORB).astype(jnp.bfloat16)
    positions = ((jnp.arange(LIST, dtype=jnp.int32) // PER)[None, :] * OWN + listed).astype(jnp.int32)
    selected = projected[positions]

    def one_box(pieces):
        coeffs, chosen = pieces
        return -jnp.dot(coeffs.astype(jnp.float32), chosen.astype(jnp.float32), precision=lax.Precision.HIGHEST)

    result = lax.map(one_box, (interp.reshape(box_total, BOX, LIST), selected))
    return result.reshape(box_total * BOX, NORB)
```

```python
import functools

import jax
import jax.numpy as jnp
from jax import lax
from jax.experimental import pallas as pl
from jax.experimental.pallas import tpu as pltpu
from jax.sharding import PartitionSpec as P

NORB = 512
LIST = 1024
OWN = 256
SLOTS = 768
LANES = 128
VMEM_LIMIT = 48 * 1024 * 1024


def vmem():
    return pl.BlockSpec(memory_space=pltpu.VMEM)


def smem():
    return pl.BlockSpec(memory_space=pltpu.SMEM)


def params():
    return pltpu.CompilerParams(vmem_limit_bytes=VMEM_LIMIT)


def pick_kernel(box_total, capacity, scalars, counts, owner_map, grid_rows, orbitals, out):
    targets = box_total * capacity
    my_box = scalars[0]
    start = jnp.int32(0)
    for b in range(box_total):
        start = start + jnp.where(b < my_box, counts[b], 0)
    stop = start + counts[my_box]
    first = start // LANES
    shift = start - first * LANES
    blocks = SLOTS // LANES + 1
    top = owner_map.shape[0] - 1
    lane = lax.broadcasted_iota(jnp.int32, (1, LANES), 1)
    turned = pltpu.roll(grid_rows[...], shift, 1)
    lane8 = lax.broadcasted_iota(jnp.int32, turned.shape, 1)
    lined = jnp.where(lane8 < shift, pltpu.roll(turned, 1, 0), turned)
    before = (
        lax.broadcasted_iota(jnp.int32, (LANES, LANES), 0)
        < lax.broadcasted_iota(jnp.int32, (LANES, LANES), 1)
    ).astype(jnp.bfloat16)
    owner_ids = lax.broadcasted_iota(jnp.int32, (box_total, LANES), 0)
    target_ids = lax.broadcasted_iota(jnp.int32, (targets, LANES), 0)
    base = jnp.zeros((box_total, 1), jnp.float32)
    found = jnp.zeros((targets, LANES), jnp.int32)
    for i in range(blocks):
        k = (first + i) * LANES + lane
        position = owner_map[pl.ds(jnp.minimum(first + i, top), 1), :]
        live = (k >= start) & (k < stop)
        owner = jnp.where(live, position // OWN, -1)
        member = (owner_ids == owner).astype(jnp.float32)
        inner = jnp.dot(member.astype(jnp.bfloat16), before, preferred_element_type=jnp.float32)
        rank = jnp.sum(member * (inner + base), axis=0, keepdims=True).astype(jnp.int32)
        base = base + jnp.sum(member, axis=1, keepdims=True)
        target = jnp.where(live, owner * capacity + rank, -1)
        found = found + jnp.where(target_ids == target, lined[i : i + 1, :] + 1, 0)
    source = jnp.sum(found.astype(jnp.float32), axis=1, keepdims=True).astype(jnp.int32) - 1
    box = orbitals.shape[0]
    step = 256
    for t in range(0, targets, step):
        hot = source[t : t + step] == lax.broadcasted_iota(jnp.int32, (step, box), 1)
        out[t : t + step, :] = jnp.dot(
            hot.astype(jnp.float32).astype(jnp.bfloat16),
            orbitals[...],
            preferred_element_type=jnp.float32,
        ).astype(jnp.bfloat16)


def place_kernel(index, rows, out):
    hot = index[...] == lax.broadcasted_iota(jnp.int32, (index.shape[0], rows.shape[0]), 1)
    out[...] = jnp.dot(
        hot.astype(jnp.float32).astype(jnp.bfloat16), rows[...], preferred_element_type=jnp.float32
    ).astype(jnp.bfloat16)


def block_kernel(row_count, scalars, left, *refs):
    right = refs[: row_count // 2]
    mirrored, coulomb, out, tile, sem = refs[row_count // 2 :]
    block, me = scalars[0], scalars[1]
    copy = pltpu.make_async_copy(coulomb.at[pl.ds(block * OWN, OWN), :], tile, sem)
    copy.start()
    total = None
    for m in range(row_count):
        columns = right[m // 2][...] if m % 2 == 0 else mirrored[m // 2]
        pair = lax.dot_general(
            left[...], columns, (((1,), (1,)), ((), ())), preferred_element_type=jnp.float32
        ).astype(jnp.bfloat16)
        if m == 0:
            copy.wait()
        place = pl.multiple_of(jnp.bitwise_xor(me, m) * OWN, OWN)
        weighted = (
            pair.astype(jnp.float32) * tile[:, pl.ds(place, OWN)].astype(jnp.float32)
        ).astype(jnp.bfloat16)
        term = jnp.dot(weighted, columns, preferred_element_type=jnp.float32)
        total = term if total is None else total + term
    out[...] = total.astype(out.dtype)


def block_sum(row_count, block, me, left, right, mirrored, coulomb, dtype):
    flops = 4 * OWN * OWN * row_count * NORB
    return pl.pallas_call(
        functools.partial(block_kernel, row_count),
        out_shape=jax.ShapeDtypeStruct((OWN, NORB), dtype),
        in_specs=[smem(), vmem()]
        + [vmem()] * (row_count // 2 + 1)
        + [pl.BlockSpec(memory_space=pl.ANY)],
        out_specs=vmem(),
        scratch_shapes=[
            pltpu.VMEM((OWN, row_count * OWN), jnp.bfloat16),
            pltpu.SemaphoreType.DMA,
        ],
        compiler_params=params(),
        cost_estimate=pl.CostEstimate(
            flops=flops, bytes_accessed=OWN * OWN * row_count * 4, transcendentals=0
        ),
    )(jnp.stack([block, me]).astype(jnp.int32), left, *right, mirrored, coulomb)


def select_kernel(others, index, own, *refs):
    out = refs[others]
    total = own[...]
    for ref in refs[:others]:
        total = total + ref[...].astype(jnp.float32)
    projected = total.astype(jnp.bfloat16)
    hot = index[...] == lax.broadcasted_iota(jnp.int32, (index.shape[0], OWN), 1)
    out[...] = jnp.dot(
        hot.astype(jnp.float32).astype(jnp.bfloat16), projected, preferred_element_type=jnp.float32
    ).astype(jnp.bfloat16)


def apply_kernel(interp, chosen, out):
    out[...] = -jnp.dot(interp[...], chosen[...], preferred_element_type=jnp.float32)


def shards(orbitals, coulomb, interp, box_counts, owner_map, grid_rows, listed):
    row_count = lax.axis_size("row")
    col_count = lax.axis_size("col")
    box_total = row_count * col_count
    point_total = OWN * box_total
    capacity = (SLOTS + box_total - 1) // box_total
    per_owner = LIST // box_total
    my_row, my_col = lax.axis_index("row"), lax.axis_index("col")
    my_box = my_row * col_count + my_col
    all_listed = lax.all_gather(listed[0], ("row", "col"), axis=0, tiled=False)
    wanted = lax.dynamic_slice(all_listed, (0, my_box * per_owner), (box_total, per_owner))
    wanted = wanted.reshape(LIST, 1)

    outgoing = pl.pallas_call(
        functools.partial(pick_kernel, box_total, capacity),
        out_shape=jax.ShapeDtypeStruct((box_total * capacity, NORB), jnp.bfloat16),
        in_specs=[smem(), smem(), vmem(), vmem(), vmem()],
        out_specs=vmem(),
        compiler_params=params(),
        cost_estimate=pl.CostEstimate(
            flops=2 * SLOTS * LIST * NORB, bytes_accessed=2 << 20, transcendentals=0
        ),
    )(
        my_box.reshape(1).astype(jnp.int32),
        box_counts,
        owner_map.reshape(point_total // LANES, LANES),
        grid_rows.reshape(grid_rows.shape[1] // LANES, LANES),
        orbitals,
    )
    received = lax.all_to_all(
        outgoing.reshape(box_total, capacity, NORB),
        ("row", "col"),
        split_axis=0,
        concat_axis=0,
        tiled=True,
    ).reshape(box_total * capacity, NORB)

    wanted_pos = my_box * OWN + jnp.arange(OWN, dtype=jnp.int32)
    all_listing = jnp.arange(point_total, dtype=jnp.int32)
    my_points = jnp.sum(
        jnp.where(owner_map[None, :] == wanted_pos[:, None], all_listing[None, :], 0), axis=1
    )
    box_ends = jnp.cumsum(box_counts)
    source = jnp.sum((my_points[:, None] >= box_ends[None, :]).astype(jnp.int32), axis=1)
    earlier = (source[:, None] == source[None, :]) & (my_points[None, :] < my_points[:, None])
    source_rank = jnp.sum(earlier.astype(jnp.int32), axis=1)
    index = (source * capacity + source_rank).reshape(OWN, 1)
    owned_rows = pl.pallas_call(
        place_kernel,
        out_shape=jax.ShapeDtypeStruct((OWN, NORB), jnp.bfloat16),
        in_specs=[vmem(), vmem()],
        out_specs=vmem(),
        compiler_params=params(),
    )(index, received)

    left = [owned_rows]
    for d in range(1, col_count):
        left.append(
            lax.ppermute(owned_rows, "col", [((i + d) % col_count, i) for i in range(col_count)])
        )
    right = [owned_rows]
    for m in range(2, row_count, 2):
        right.append(lax.ppermute(owned_rows, "row", [(i, i ^ m) for i in range(row_count)]))
    mirrored = lax.ppermute(jnp.stack(right), "row", [(i, i ^ 1) for i in range(row_count)])

    sums = []
    for d in range(col_count):
        block = lax.rem(my_col + d, col_count)
        dtype = jnp.float32 if d == 0 else jnp.bfloat16
        sums.append(
            block_sum(row_count, block, my_row, left[d], right, mirrored, coulomb, dtype)
        )
    arrived = [
        lax.ppermute(sums[d], "col", [(i, (i + d) % col_count) for i in range(col_count)])
        for d in range(1, col_count)
    ]
    picked = pl.pallas_call(
        functools.partial(select_kernel, len(arrived)),
        out_shape=jax.ShapeDtypeStruct((LIST, NORB), jnp.bfloat16),
        in_specs=[vmem()] * (2 + len(arrived)),
        out_specs=vmem(),
        compiler_params=params(),
    )(wanted, sums[0], *arrived)
    chosen = lax.all_to_all(
        picked.reshape(box_total, per_owner, NORB),
        ("row", "col"),
        split_axis=0,
        concat_axis=0,
        tiled=True,
    ).reshape(LIST, NORB)
    box = interp.shape[0]
    step = 256
    return pl.pallas_call(
        apply_kernel,
        grid=(box // step,),
        out_shape=jax.ShapeDtypeStruct((box, NORB), jnp.float32),
        in_specs=[
            pl.BlockSpec((step, LIST), lambda i: (i, 0)),
            pl.BlockSpec((LIST, NORB), lambda i: (0, 0)),
        ],
        out_specs=pl.BlockSpec((step, NORB), lambda i: (i, 0)),
        compiler_params=params(),
    )(interp, chosen)


def solution(mesh):
    return jax.shard_map(
        shards,
        mesh=mesh,
        in_specs=(
            P(("row", "col"), None),
            P("row", "col"),
            P(("row", "col"), None),
            P(),
            P(),
            P(("row", "col"), None),
            P(("row", "col"), None),
        ),
        out_specs=P(("row", "col"), None),
        check_vma=False,
    )
```

```python
import functools

import jax
import jax.numpy as jnp
from jax import lax
from jax.experimental import pallas as pl
from jax.experimental.pallas import tpu as pltpu
from jax.sharding import PartitionSpec as P

NORB = 512
LIST = 1024
OWN = 256
SLOTS = 768
LANES = 128
VMEM_LIMIT = 48 * 1024 * 1024
PICK_LIMIT = 60 * 1024 * 1024


def vmem():
    return pl.BlockSpec(memory_space=pltpu.VMEM)


def smem():
    return pl.BlockSpec(memory_space=pltpu.SMEM)


def hbm():
    return pl.BlockSpec(memory_space=pltpu.HBM)


def params(limit=VMEM_LIMIT):
    return pltpu.CompilerParams(vmem_limit_bytes=limit)


def pick_kernel(
    box_total, capacity, scalars, counts, owner_hbm, grid_hbm, orbitals_hbm, out,
    owner_map, grid_rows, orbitals, sems,
):
    copies = [
        pltpu.make_async_copy(source, target, sems.at[n])
        for n, (source, target) in enumerate(
            [(grid_hbm, grid_rows), (owner_hbm, owner_map), (orbitals_hbm, orbitals)]
        )
    ]
    for copy in copies:
        copy.start()
    targets = box_total * capacity
    my_box = scalars[0]
    start = jnp.int32(0)
    for b in range(box_total):
        start = start + jnp.where(b < my_box, counts[b], 0)
    stop = start + counts[my_box]
    first = start // LANES
    shift = start - first * LANES
    blocks = SLOTS // LANES + 1
    top = owner_map.shape[0] - 1
    lane = lax.broadcasted_iota(jnp.int32, (1, LANES), 1)
    copies[0].wait()
    copies[1].wait()
    turned = pltpu.roll(grid_rows[...], shift, 1)
    lane8 = lax.broadcasted_iota(jnp.int32, turned.shape, 1)
    lined = jnp.where(lane8 < shift, pltpu.roll(turned, 1, 0), turned)
    before = (
        lax.broadcasted_iota(jnp.int32, (LANES, LANES), 0)
        < lax.broadcasted_iota(jnp.int32, (LANES, LANES), 1)
    ).astype(jnp.bfloat16)
    owner_ids = lax.broadcasted_iota(jnp.int32, (box_total, LANES), 0)
    target_ids = lax.broadcasted_iota(jnp.int32, (targets, LANES), 0)
    base = jnp.zeros((box_total, 1), jnp.float32)
    found = jnp.zeros((targets, LANES), jnp.int32)
    for i in range(blocks):
        k = (first + i) * LANES + lane
        position = owner_map[pl.ds(jnp.minimum(first + i, top), 1), :]
        live = (k >= start) & (k < stop)
        owner = jnp.where(live, position // OWN, -1)
        member = (owner_ids == owner).astype(jnp.float32)
        inner = jnp.dot(member.astype(jnp.bfloat16), before, preferred_element_type=jnp.float32)
        rank = jnp.sum(member * (inner + base), axis=0, keepdims=True).astype(jnp.int32)
        base = base + jnp.sum(member, axis=1, keepdims=True)
        target = jnp.where(live, owner * capacity + rank, -1)
        found = found + jnp.where(target_ids == target, lined[i : i + 1, :] + 1, 0)
    source = jnp.sum(found.astype(jnp.float32), axis=1, keepdims=True).astype(jnp.int32) - 1
    box = orbitals.shape[0]
    step = 256
    copies[2].wait()
    for t in range(0, targets, step):
        hot = source[t : t + step] == lax.broadcasted_iota(jnp.int32, (step, box), 1)
        out[t : t + step, :] = jnp.dot(
            hot.astype(jnp.float32).astype(jnp.bfloat16),
            orbitals[...],
            preferred_element_type=jnp.float32,
        ).astype(jnp.bfloat16)


def place_kernel(index, rows, out):
    hot = index[...] == lax.broadcasted_iota(jnp.int32, (index.shape[0], rows.shape[0]), 1)
    out[...] = jnp.dot(
        hot.astype(jnp.float32).astype(jnp.bfloat16), rows[...], preferred_element_type=jnp.float32
    ).astype(jnp.bfloat16)


def block_kernel(masks, scalars, left, *refs):
    columns = refs[: len(masks)]
    coulomb, *earlier, out, right, tile, weighted, sems = refs[len(masks) :]
    rows = pl.ds(pl.multiple_of(scalars[0] * OWN, OWN), OWN)
    copies = []
    for n, mask in enumerate(masks):
        place = pl.multiple_of(jnp.bitwise_xor(scalars[1], mask) * OWN, OWN)
        copies.append(
            pltpu.make_async_copy(
                coulomb.at[rows, pl.ds(place, OWN)],
                tile.at[:, n * OWN : (n + 1) * OWN],
                sems.at[n],
            )
        )
        copies[-1].start()
    for n, ref in enumerate(columns):
        right[n * OWN : (n + 1) * OWN, :] = ref[...]
    step = 512
    for t in range(0, right.shape[0], step):
        weighted[:, t : t + step] = lax.dot_general(
            left[...],
            right[t : t + step, :],
            (((1,), (1,)), ((), ())),
            preferred_element_type=jnp.float32,
        ).astype(jnp.bfloat16)
    for copy in copies:
        copy.wait()
    for t in range(0, right.shape[0], step):
        pair = weighted[:, t : t + step].astype(jnp.float32)
        weighted[:, t : t + step] = (
            pair * tile[:, t : t + step].astype(jnp.float32)
        ).astype(jnp.bfloat16)
    total = jnp.dot(weighted[...], right[...], preferred_element_type=jnp.float32)
    for ref in earlier:
        total = total + ref[...]
    out[...] = total.astype(out.dtype)


def block_sum(masks, block, me, left, right, coulomb, dtype, earlier=()):
    columns = len(masks) * OWN
    return pl.pallas_call(
        functools.partial(block_kernel, masks),
        out_shape=jax.ShapeDtypeStruct((OWN, NORB), dtype),
        in_specs=[smem(), vmem()]
        + [vmem()] * len(masks)
        + [hbm()]
        + [vmem()] * len(earlier),
        out_specs=vmem(),
        scratch_shapes=[
            pltpu.VMEM((columns, NORB), jnp.bfloat16),
            pltpu.VMEM((OWN, columns), jnp.bfloat16),
            pltpu.VMEM((OWN, columns), jnp.bfloat16),
            pltpu.SemaphoreType.DMA((len(masks),)),
        ],
        compiler_params=params(),
        cost_estimate=pl.CostEstimate(flops=0, bytes_accessed=0, transcendentals=0),
    )(
        jnp.stack([block, me]).astype(jnp.int32),
        left,
        *[right[mask] for mask in masks],
        coulomb,
        *earlier,
    )


def select_kernel(others, index, own, *refs):
    boxes, per_owner = index.shape
    spread = jnp.broadcast_to(index[...][:, None, :], (boxes, per_owner, per_owner))
    diagonal = lax.broadcasted_iota(jnp.int32, spread.shape, 1) == lax.broadcasted_iota(
        jnp.int32, spread.shape, 2
    )
    picks = jnp.sum(jnp.where(diagonal, spread, 0).astype(jnp.float32), axis=2, keepdims=True)
    picks = picks.reshape(boxes * per_owner, 1).astype(jnp.int32)
    out = refs[others]
    total = own[...]
    for ref in refs[:others]:
        total = total + ref[...].astype(jnp.float32)
    projected = total.astype(jnp.bfloat16)
    hot = picks == lax.broadcasted_iota(jnp.int32, (boxes * per_owner, OWN), 1)
    out[...] = jnp.dot(
        hot.astype(jnp.float32).astype(jnp.bfloat16), projected, preferred_element_type=jnp.float32
    ).astype(jnp.bfloat16)


def apply_kernel(interp, chosen, out):
    out[...] = -jnp.dot(interp[...], chosen[...], preferred_element_type=jnp.float32)


def shards(orbitals, coulomb, interp, box_counts, owner_map, grid_rows, listed):
    row_count = lax.axis_size("row")
    col_count = lax.axis_size("col")
    box_total = row_count * col_count
    point_total = OWN * box_total
    capacity = (SLOTS + box_total - 1) // box_total
    per_owner = LIST // box_total
    my_row, my_col = lax.axis_index("row"), lax.axis_index("col")
    my_box = my_row * col_count + my_col
    outgoing = pl.pallas_call(
        functools.partial(pick_kernel, box_total, capacity),
        out_shape=jax.ShapeDtypeStruct((box_total * capacity, NORB), jnp.bfloat16),
        in_specs=[smem(), smem(), hbm(), hbm(), hbm()],
        out_specs=vmem(),
        scratch_shapes=[
            pltpu.VMEM((point_total // LANES, LANES), jnp.int32),
            pltpu.VMEM((grid_rows.shape[1] // LANES, LANES), jnp.int32),
            pltpu.VMEM(orbitals.shape, jnp.bfloat16),
            pltpu.SemaphoreType.DMA((3,)),
        ],
        compiler_params=params(PICK_LIMIT),
        cost_estimate=pl.CostEstimate(
            flops=2 * SLOTS * LIST * NORB, bytes_accessed=2 << 20, transcendentals=0
        ),
    )(
        my_box.reshape(1).astype(jnp.int32),
        box_counts,
        owner_map.reshape(point_total // LANES, LANES),
        grid_rows.reshape(grid_rows.shape[1] // LANES, LANES),
        orbitals,
    )
    received = lax.all_to_all(
        outgoing.reshape(box_total, capacity, NORB),
        ("row", "col"),
        split_axis=0,
        concat_axis=0,
        tiled=True,
    ).reshape(box_total * capacity, NORB)

    wanted_pos = my_box * OWN + jnp.arange(OWN, dtype=jnp.int32)
    all_listing = jnp.arange(point_total, dtype=jnp.int32)
    my_points = jnp.sum(
        jnp.where(owner_map[None, :] == wanted_pos[:, None], all_listing[None, :], 0), axis=1
    )
    box_ends = jnp.cumsum(box_counts)
    source = jnp.sum((my_points[:, None] >= box_ends[None, :]).astype(jnp.int32), axis=1)
    earlier = (source[:, None] == source[None, :]) & (my_points[None, :] < my_points[:, None])
    source_rank = jnp.sum(earlier.astype(jnp.int32), axis=1)
    index = (source * capacity + source_rank).reshape(OWN, 1)
    owned_rows = pl.pallas_call(
        place_kernel,
        out_shape=jax.ShapeDtypeStruct((OWN, NORB), jnp.bfloat16),
        in_specs=[vmem(), vmem()],
        out_specs=vmem(),
        compiler_params=params(),
    )(index, received)

    left = [owned_rows]
    for d in range(1, col_count):
        left.append(
            lax.ppermute(owned_rows, "col", [((i + d) % col_count, i) for i in range(col_count)])
        )
    def flip(rows, mask):
        return lax.ppermute(rows, "row", [(i, i ^ mask) for i in range(row_count)])

    even, odd = list(range(0, row_count, 2)), list(range(1, row_count, 2))
    right = {0: owned_rows}
    for mask in even[1:]:
        right[mask] = flip(owned_rows, mask)
    for mask in even:
        right[mask + 1] = flip(right[mask], 1)

    def block_of(d):
        return lax.rem(my_col + d, col_count)

    def run(masks, d, dtype, earlier=()):
        return block_sum(masks, block_of(d), my_row, left[d], right, coulomb, dtype, earlier)

    sums = [None] * col_count
    first = run(even, 1, jnp.float32)
    sums[1] = run(odd, 1, jnp.bfloat16, (first,))
    for d in range(2, col_count):
        sums[d] = run(even + odd, d, jnp.bfloat16)
    sums[0] = run(even + odd, 0, jnp.float32)
    arrived = [
        lax.ppermute(sums[d], "col", [(i, (i + d) % col_count) for i in range(col_count)])
        for d in range(1, col_count)
    ]
    own_sum, asked = lax.optimization_barrier((sums[0], listed[0]))
    wanted = lax.all_to_all(
        asked.reshape(box_total, per_owner),
        ("row", "col"),
        split_axis=0,
        concat_axis=0,
        tiled=True,
    )
    picked = pl.pallas_call(
        functools.partial(select_kernel, len(arrived)),
        out_shape=jax.ShapeDtypeStruct((LIST, NORB), jnp.bfloat16),
        in_specs=[vmem()] * (2 + len(arrived)),
        out_specs=vmem(),
        compiler_params=params(),
    )(wanted, own_sum, *arrived)
    chosen = lax.all_to_all(
        picked.reshape(box_total, per_owner, NORB),
        ("row", "col"),
        split_axis=0,
        concat_axis=0,
        tiled=True,
    ).reshape(LIST, NORB)
    box = interp.shape[0]
    step = 256
    return pl.pallas_call(
        apply_kernel,
        grid=(box // step,),
        out_shape=jax.ShapeDtypeStruct((box, NORB), jnp.float32),
        in_specs=[
            pl.BlockSpec((step, LIST), lambda i: (i, 0)),
            pl.BlockSpec((LIST, NORB), lambda i: (0, 0)),
        ],
        out_specs=pl.BlockSpec((step, NORB), lambda i: (i, 0)),
        compiler_params=params(),
    )(interp, chosen)


def solution(mesh):
    return jax.shard_map(
        shards,
        mesh=mesh,
        in_specs=(
            P(("row", "col"), None),
            P("row", "col"),
            P(("row", "col"), None),
            P(),
            P(),
            P(("row", "col"), None),
            P(("row", "col"), None),
        ),
        out_specs=P(("row", "col"), None),
        check_vma=False,
    )
```

```python
import functools

import jax
import jax.numpy as jnp
from jax import lax
from jax.experimental import pallas as pl
from jax.experimental.pallas import tpu as pltpu
from jax.sharding import PartitionSpec as P

NORB = 512
LIST = 1024
OWN = 256
SLOTS = 768
LANES = 128
VMEM_LIMIT = 48 * 1024 * 1024
PICK_LIMIT = 60 * 1024 * 1024


def vmem():
    return pl.BlockSpec(memory_space=pltpu.VMEM)


def smem():
    return pl.BlockSpec(memory_space=pltpu.SMEM)


def hbm():
    return pl.BlockSpec(memory_space=pltpu.HBM)


def params(limit=VMEM_LIMIT):
    return pltpu.CompilerParams(vmem_limit_bytes=limit)


def pick_kernel(
    box_total, capacity, scalars, counts, listed, owner_hbm, grid_hbm, orbitals_hbm, out,
    owner_map, grid_rows, orbitals, sems,
):
    copies = [
        pltpu.make_async_copy(source, target, sems.at[n])
        for n, (source, target) in enumerate(
            [(grid_hbm, grid_rows), (owner_hbm, owner_map), (orbitals_hbm, orbitals)]
        )
    ]
    for copy in copies:
        copy.start()
    targets = box_total * capacity
    my_box = scalars[0]
    start = jnp.int32(0)
    for b in range(box_total):
        start = start + jnp.where(b < my_box, counts[b], 0)
    stop = start + counts[my_box]
    first = start // LANES
    shift = start - first * LANES
    blocks = SLOTS // LANES + 1
    top = owner_map.shape[0] - 1
    lane = lax.broadcasted_iota(jnp.int32, (1, LANES), 1)
    copies[0].wait()
    copies[1].wait()
    turned = pltpu.roll(grid_rows[...], shift, 1)
    lane8 = lax.broadcasted_iota(jnp.int32, turned.shape, 1)
    lined = jnp.where(lane8 < shift, pltpu.roll(turned, 1, 0), turned)
    before = (
        lax.broadcasted_iota(jnp.int32, (LANES, LANES), 0)
        < lax.broadcasted_iota(jnp.int32, (LANES, LANES), 1)
    ).astype(jnp.bfloat16)
    owner_ids = lax.broadcasted_iota(jnp.int32, (box_total, LANES), 0)
    target_ids = lax.broadcasted_iota(jnp.int32, (targets, LANES), 0)
    base = jnp.zeros((box_total, 1), jnp.float32)
    found = jnp.zeros((targets, LANES), jnp.int32)
    for i in range(blocks):
        k = (first + i) * LANES + lane
        position = owner_map[pl.ds(jnp.minimum(first + i, top), 1), :]
        live = (k >= start) & (k < stop)
        owner = jnp.where(live, position // OWN, -1)
        member = (owner_ids == owner).astype(jnp.float32)
        inner = jnp.dot(member.astype(jnp.bfloat16), before, preferred_element_type=jnp.float32)
        rank = jnp.sum(member * (inner + base), axis=0, keepdims=True).astype(jnp.int32)
        base = base + jnp.sum(member, axis=1, keepdims=True)
        target = jnp.where(live, owner * capacity + rank, -1)
        found = found + jnp.where(target_ids == target, lined[i : i + 1, :] + 1, 0)
    source = jnp.sum(found.astype(jnp.float32), axis=1, keepdims=True).astype(jnp.int32) - 1
    per_owner = LIST // box_total
    fold = LANES // per_owner
    spread = jnp.broadcast_to(listed[...][:, None, :], (LIST // LANES, fold, LANES))
    spread = spread.reshape(box_total, LANES)
    phase = lax.broadcasted_iota(jnp.int32, spread.shape, 0) % fold
    indices = spread
    for q in range(1, fold):
        indices = jnp.where(phase == q, pltpu.roll(spread, LANES - q * per_owner, 1), indices)
    indices = indices.astype(jnp.float32).astype(jnp.bfloat16)
    tail = out.shape[1] - capacity * (NORB // LANES)
    out[:, capacity * (NORB // LANES) :, :] = jnp.broadcast_to(
        indices[:, None, :], (box_total, tail, LANES)
    )
    box = orbitals.shape[0]
    step = targets // 4
    copies[2].wait()
    for t in range(0, targets, step):
        hot = source[t : t + step] == lax.broadcasted_iota(jnp.int32, (step, box), 1)
        rows = jnp.dot(
            hot.astype(jnp.float32).astype(jnp.bfloat16),
            orbitals[...],
            preferred_element_type=jnp.float32,
        ).astype(jnp.bfloat16)
        first_owner = t // capacity
        for c in range(NORB // LANES):
            out[
                first_owner : first_owner + step // capacity, c * capacity : (c + 1) * capacity, :
            ] = rows[:, c * LANES : (c + 1) * LANES].reshape(step // capacity, capacity, LANES)


def place_kernel(capacity, index, received, out, wanted):
    boxes = received.shape[0]
    rows = jnp.concatenate(
        [
            received[:, c * capacity : (c + 1) * capacity, :].reshape(boxes * capacity, LANES)
            for c in range(NORB // LANES)
        ],
        axis=1,
    )
    hot = index[...] == lax.broadcasted_iota(jnp.int32, (index.shape[0], rows.shape[0]), 1)
    out[...] = jnp.dot(
        hot.astype(jnp.float32).astype(jnp.bfloat16), rows, preferred_element_type=jnp.float32
    ).astype(jnp.bfloat16)
    tail = received[:, capacity * (NORB // LANES) :, :].astype(jnp.float32)
    wanted[...] = tail[:, 0, :].astype(jnp.int32)


def join_kernel(*refs):
    out, at = refs[-1], 0
    for ref in refs[:-1]:
        out[at : at + ref.shape[0], :] = ref[...]
        at += ref.shape[0]


def hold_kernel(*refs):
    count = len(refs) // 2
    for source, target in zip(refs[:count], refs[count:]):
        target[...] = source[...]


def pair_block(left, right):
    return lax.dot_general(
        left, right, (((1,), (1,)), ((), ())), preferred_element_type=jnp.float32
    ).astype(jnp.bfloat16)


def order_kernel(scalars, even, odd, out):
    for parity, ref in enumerate((even, odd)):
        for n in range(ref.shape[0] // OWN):
            place = jnp.bitwise_xor(scalars[0], 2 * n + parity) * OWN
            out[pl.ds(pl.multiple_of(place, OWN), OWN), :] = ref[n * OWN : (n + 1) * OWN, :]


def block_kernel(scalars, left, right, coulomb, out, tile, weighted, sem):
    source = pl.ds(pl.multiple_of(scalars[1] * OWN, OWN), OWN)
    copy = pltpu.make_async_copy(coulomb.at[source, :], tile, sem)
    copy.start()
    step = 512
    for t in range(0, right.shape[0], step):
        weighted[:, t : t + step] = pair_block(left[...], right[t : t + step, :])
    copy.wait()
    for t in range(0, right.shape[0], step):
        pair = weighted[:, t : t + step].astype(jnp.float32)
        weighted[:, t : t + step] = (
            pair * tile[:, t : t + step].astype(jnp.float32)
        ).astype(jnp.bfloat16)
    out[...] = jnp.dot(
        weighted[...], right[...], preferred_element_type=jnp.float32
    ).astype(out.dtype)


def block_sum(numbers, left, right, coulomb, dtype):
    columns = right.shape[0]
    return local(
        block_kernel,
        jax.ShapeDtypeStruct((OWN, NORB), dtype),
        numbers,
        left,
        right,
        coulomb,
        flops=4 * OWN * columns * NORB,
        far=3,
        scratch=[
            pltpu.VMEM((OWN, columns), jnp.bfloat16),
            pltpu.VMEM((OWN, columns), jnp.bfloat16),
            pltpu.SemaphoreType.DMA,
        ],
    )


def local(kernel, out, *args, flops=0, far=None, scratch=()):
    def spec(n, a):
        if n == far:
            return hbm()
        return smem() if a.ndim == 1 else vmem()

    return pl.pallas_call(
        kernel,
        out_shape=out,
        in_specs=[spec(n, a) for n, a in enumerate(args)],
        out_specs=jax.tree.map(lambda _: vmem(), out),
        scratch_shapes=scratch,
        compiler_params=params(),
        cost_estimate=pl.CostEstimate(flops=flops, bytes_accessed=0, transcendentals=0),
    )(*args)


def select_kernel(others, per_owner, index, own, *refs):
    boxes = index.shape[0]
    spread = jnp.broadcast_to(index[...][:, None, :], (boxes, per_owner, LANES))
    diagonal = lax.broadcasted_iota(jnp.int32, spread.shape, 1) == lax.broadcasted_iota(
        jnp.int32, spread.shape, 2
    )
    picks = jnp.sum(jnp.where(diagonal, spread, 0).astype(jnp.float32), axis=2, keepdims=True)
    picks = picks.reshape(boxes * per_owner, 1).astype(jnp.int32)
    out = refs[-1]
    totals, rows = [], refs[0].shape[0]
    for n in range(OWN // rows):
        total = own[n * rows : (n + 1) * rows, :]
        for ref in refs[n * others : (n + 1) * others]:
            total = total + ref[...].astype(jnp.float32)
        totals.append(total.astype(jnp.bfloat16))
    projected = jnp.concatenate(totals)
    hot = picks == lax.broadcasted_iota(jnp.int32, (boxes * per_owner, OWN), 1)
    out[...] = jnp.dot(
        hot.astype(jnp.float32).astype(jnp.bfloat16), projected, preferred_element_type=jnp.float32
    ).astype(jnp.bfloat16)


def apply_kernel(interp, chosen, out):
    out[...] = -jnp.dot(interp[...], chosen[...], preferred_element_type=jnp.float32)


def shards(orbitals, coulomb, interp, box_counts, owner_map, grid_rows, listed):
    row_count = lax.axis_size("row")
    col_count = lax.axis_size("col")
    box_total = row_count * col_count
    point_total = OWN * box_total
    capacity = (SLOTS + box_total - 1) // box_total
    per_owner = LIST // box_total
    my_row, my_col = lax.axis_index("row"), lax.axis_index("col")
    my_box = my_row * col_count + my_col
    packed = capacity * (NORB // LANES)
    packed = (packed // 8 + 1) * 8
    outgoing = pl.pallas_call(
        functools.partial(pick_kernel, box_total, capacity),
        out_shape=jax.ShapeDtypeStruct((box_total, packed, LANES), jnp.bfloat16),
        in_specs=[smem(), smem(), vmem(), hbm(), hbm(), hbm()],
        out_specs=vmem(),
        scratch_shapes=[
            pltpu.VMEM((point_total // LANES, LANES), jnp.int32),
            pltpu.VMEM((grid_rows.shape[1] // LANES, LANES), jnp.int32),
            pltpu.VMEM(orbitals.shape, jnp.bfloat16),
            pltpu.SemaphoreType.DMA((3,)),
        ],
        compiler_params=params(PICK_LIMIT),
        cost_estimate=pl.CostEstimate(
            flops=2 * SLOTS * LIST * NORB, bytes_accessed=2 << 20, transcendentals=0
        ),
    )(
        my_box.reshape(1).astype(jnp.int32),
        box_counts,
        listed.reshape(LIST // LANES, LANES),
        owner_map.reshape(point_total // LANES, LANES),
        grid_rows.reshape(grid_rows.shape[1] // LANES, LANES),
        orbitals,
    )
    received = lax.all_to_all(
        outgoing, ("row", "col"), split_axis=0, concat_axis=0, tiled=True
    )

    wanted_pos = my_box * OWN + jnp.arange(OWN, dtype=jnp.int32)
    all_listing = jnp.arange(point_total, dtype=jnp.int32)
    my_points = jnp.sum(
        jnp.where(owner_map[None, :] == wanted_pos[:, None], all_listing[None, :], 0), axis=1
    )
    box_ends = jnp.cumsum(box_counts)
    source = jnp.sum((my_points[:, None] >= box_ends[None, :]).astype(jnp.int32), axis=1)
    earlier = (source[:, None] == source[None, :]) & (my_points[None, :] < my_points[:, None])
    source_rank = jnp.sum(earlier.astype(jnp.int32), axis=1)
    index = (source * capacity + source_rank).reshape(OWN, 1)
    owned_rows, wanted = pl.pallas_call(
        functools.partial(place_kernel, capacity),
        out_shape=(
            jax.ShapeDtypeStruct((OWN, NORB), jnp.bfloat16),
            jax.ShapeDtypeStruct((box_total, LANES), jnp.int32),
        ),
        in_specs=[vmem(), vmem()],
        out_specs=(vmem(), vmem()),
        compiler_params=params(),
    )(index, received)

    def swap(rows, mask):
        return lax.ppermute(rows, "col", [(i, i ^ mask) for i in range(col_count)])

    def flip(rows, mask):
        return lax.ppermute(rows, "row", [(i, i ^ mask) for i in range(row_count)])

    left = {0: owned_rows}
    for mask in range(1, col_count):
        if mask & (mask - 1) == 0:
            left[mask] = swap(owned_rows, mask)

    blocks = {0: [owned_rows]}
    whole = {0: owned_rows}
    half = OWN // 2
    for mask in range(2, row_count, 2):
        bits = [1 << b for b in range(1, mask.bit_length()) if mask >> b & 1]
        if len(bits) == 1:
            blocks[mask] = [flip(owned_rows, mask)]
        else:
            low, high = bits[0], bits[-1]
            blocks[mask] = [
                flip(whole[mask ^ high][:half], high),
                flip(whole[mask ^ low][half:], low),
            ]
        whole[mask] = jnp.concatenate(blocks[mask])
    pieces = [piece for mask in range(0, row_count, 2) for piece in blocks[mask]]
    shape = jax.ShapeDtypeStruct
    even = local(join_kernel, shape((row_count // 2 * OWN, NORB), jnp.bfloat16), *pieces)
    odd = flip(even, 1)
    direct = [mask for mask in left if mask]
    held = local(
        hold_kernel,
        tuple(shape(owned_rows.shape, owned_rows.dtype) for _ in direct),
        *[left[mask] for mask in direct],
        flops=20 * 10**9,
    )
    *held, odd = lax.optimization_barrier((*held, odd))
    left.update(zip(direct, held))
    for mask in range(1, col_count):
        if mask not in left:
            low = mask & -mask
            left[mask] = swap(left[mask ^ low], low)

    def numbers(mask):
        return jnp.stack([my_row, jnp.bitwise_xor(my_col, mask)]).astype(jnp.int32)

    right = local(
        order_kernel, shape((row_count * OWN, NORB), jnp.bfloat16), numbers(0), even, odd
    )

    def partial_sum(mask, dtype):
        return block_sum(numbers(mask), left[mask], right, coulomb, dtype)

    arrived = []
    for mask in sorted(range(1, col_count), key=lambda m: (m & 1, m)):
        arrived.append(swap(partial_sum(mask, jnp.bfloat16), mask))
    own_sum = partial_sum(0, jnp.float32)
    picked = pl.pallas_call(
        functools.partial(select_kernel, col_count - 1, per_owner),
        out_shape=jax.ShapeDtypeStruct((LIST, NORB), jnp.bfloat16),
        in_specs=[vmem()] * (2 + len(arrived)),
        out_specs=vmem(),
        compiler_params=params(),
    )(wanted, own_sum, *arrived)
    chosen = lax.all_to_all(
        picked.reshape(box_total, per_owner, NORB),
        ("row", "col"),
        split_axis=0,
        concat_axis=0,
        tiled=True,
    ).reshape(LIST, NORB)
    box = interp.shape[0]
    step = 256
    return pl.pallas_call(
        apply_kernel,
        grid=(box // step,),
        out_shape=jax.ShapeDtypeStruct((box, NORB), jnp.float32),
        in_specs=[
            pl.BlockSpec((step, LIST), lambda i: (i, 0)),
            pl.BlockSpec((LIST, NORB), lambda i: (0, 0)),
        ],
        out_specs=pl.BlockSpec((step, NORB), lambda i: (i, 0)),
        compiler_params=params(),
    )(interp, chosen)


def solution(mesh):
    return jax.shard_map(
        shards,
        mesh=mesh,
        in_specs=(
            P(("row", "col"), None),
            P("row", "col"),
            P(("row", "col"), None),
            P(),
            P(),
            P(("row", "col"), None),
            P(("row", "col"), None),
        ),
        out_specs=P(("row", "col"), None),
        check_vma=False,
    )
```

```python
import functools

import jax
import jax.numpy as jnp
from jax import lax
from jax.experimental import pallas as pl
from jax.experimental.pallas import tpu as pltpu
from jax.sharding import PartitionSpec as P

NORB = 512
LIST = 1024
OWN = 256
SLOTS = 768
LANES = 128
VMEM_LIMIT = 48 * 1024 * 1024
PICK_LIMIT = 60 * 1024 * 1024


def vmem():
    return pl.BlockSpec(memory_space=pltpu.VMEM)


def smem():
    return pl.BlockSpec(memory_space=pltpu.SMEM)


def hbm():
    return pl.BlockSpec(memory_space=pltpu.HBM)


def params(limit=VMEM_LIMIT):
    return pltpu.CompilerParams(vmem_limit_bytes=limit)


def pick_kernel(
    box_total, capacity, counts_hbm, grid_hbm, owner_hbm, listed_hbm, orbitals_hbm, out,
    counts, grid_rows, owner_map, listed, orbitals, sems,
):
    copies = [
        pltpu.make_async_copy(source, target, sems.at[n])
        for n, (source, target) in enumerate(
            [
                (counts_hbm, counts),
                (grid_hbm, grid_rows),
                (owner_hbm, owner_map),
                (listed_hbm, listed),
                (orbitals_hbm, orbitals),
            ]
        )
    ]
    for copy in copies:
        copy.start()
    targets = box_total * capacity
    my_box = lax.axis_index("row") * lax.axis_size("col") + lax.axis_index("col")
    copies[0].wait()
    start = jnp.int32(0)
    for b in range(box_total):
        start = start + jnp.where(b < my_box, counts[b], 0)
    stop = start + counts[my_box]
    first = start // LANES
    shift = start - first * LANES
    blocks = SLOTS // LANES + 1
    top = owner_map.shape[0] - 1
    lane = lax.broadcasted_iota(jnp.int32, (1, LANES), 1)
    copies[1].wait()
    copies[2].wait()
    turned = pltpu.roll(grid_rows[...], shift, 1)
    lane8 = lax.broadcasted_iota(jnp.int32, turned.shape, 1)
    lined = jnp.where(lane8 < shift, pltpu.roll(turned, 1, 0), turned)
    before = (
        lax.broadcasted_iota(jnp.int32, (LANES, LANES), 0)
        < lax.broadcasted_iota(jnp.int32, (LANES, LANES), 1)
    ).astype(jnp.bfloat16)
    owner_ids = lax.broadcasted_iota(jnp.int32, (box_total, LANES), 0)
    target_ids = lax.broadcasted_iota(jnp.int32, (targets, LANES), 0)
    base = jnp.zeros((box_total, 1), jnp.float32)
    found = jnp.zeros((targets, LANES), jnp.int32)
    for i in range(blocks):
        k = (first + i) * LANES + lane
        position = owner_map[pl.ds(jnp.minimum(first + i, top), 1), :]
        live = (k >= start) & (k < stop)
        owner = jnp.where(live, position // OWN, -1)
        member = (owner_ids == owner).astype(jnp.float32)
        inner = jnp.dot(member.astype(jnp.bfloat16), before, preferred_element_type=jnp.float32)
        rank = jnp.sum(member * (inner + base), axis=0, keepdims=True).astype(jnp.int32)
        base = base + jnp.sum(member, axis=1, keepdims=True)
        target = jnp.where(live, owner * capacity + rank, -1)
        found = found + jnp.where(target_ids == target, lined[i : i + 1, :] + 1, 0)
    source = jnp.sum(found.astype(jnp.float32), axis=1, keepdims=True).astype(jnp.int32) - 1
    copies[3].wait()
    per_owner = LIST // box_total
    fold = LANES // per_owner
    spread = jnp.broadcast_to(listed[...][:, None, :], (LIST // LANES, fold, LANES))
    spread = spread.reshape(box_total, LANES)
    phase = lax.broadcasted_iota(jnp.int32, spread.shape, 0) % fold
    indices = spread
    for q in range(1, fold):
        indices = jnp.where(phase == q, pltpu.roll(spread, LANES - q * per_owner, 1), indices)
    indices = indices.astype(jnp.float32).astype(jnp.bfloat16)
    tail = out.shape[1] - capacity * (NORB // LANES)
    out[:, capacity * (NORB // LANES) :, :] = jnp.broadcast_to(
        indices[:, None, :], (box_total, tail, LANES)
    )
    box = orbitals.shape[0]
    step = targets // 4
    copies[4].wait()
    for t in range(0, targets, step):
        hot = source[t : t + step] == lax.broadcasted_iota(jnp.int32, (step, box), 1)
        rows = jnp.dot(
            hot.astype(jnp.float32).astype(jnp.bfloat16),
            orbitals[...],
            preferred_element_type=jnp.float32,
        ).astype(jnp.bfloat16)
        first_owner = t // capacity
        for c in range(NORB // LANES):
            out[
                first_owner : first_owner + step // capacity, c * capacity : (c + 1) * capacity, :
            ] = rows[:, c * LANES : (c + 1) * LANES].reshape(step // capacity, capacity, LANES)


def place_kernel(capacity, index, received, out, wanted):
    boxes = received.shape[0]
    rows = jnp.concatenate(
        [
            received[:, c * capacity : (c + 1) * capacity, :].reshape(boxes * capacity, LANES)
            for c in range(NORB // LANES)
        ],
        axis=1,
    )
    hot = index[...] == lax.broadcasted_iota(jnp.int32, (index.shape[0], rows.shape[0]), 1)
    out[...] = jnp.dot(
        hot.astype(jnp.float32).astype(jnp.bfloat16), rows, preferred_element_type=jnp.float32
    ).astype(jnp.bfloat16)
    tail = received[:, capacity * (NORB // LANES) :, :].astype(jnp.float32)
    wanted[...] = tail[:, 0, :].astype(jnp.int32)


def join_kernel(*refs):
    out, at = refs[-1], 0
    for ref in refs[:-1]:
        out[at : at + ref.shape[0], :] = ref[...]
        at += ref.shape[0]


def hold_kernel(*refs):
    count = len(refs) // 2
    for source, target in zip(refs[:count], refs[count:]):
        target[...] = source[...]


def pair_block(left, right):
    return lax.dot_general(
        left, right, (((1,), (1,)), ((), ())), preferred_element_type=jnp.float32
    ).astype(jnp.bfloat16)


def order_kernel(masks, scalars, *refs):
    pieces, out = refs[:-1], refs[-1]
    places = [mask ^ parity for parity in (0, 1) for mask in masks]
    for ref in pieces:
        for n in range(ref.shape[0] // OWN):
            place = jnp.bitwise_xor(scalars[0], places.pop(0)) * OWN
            out[pl.ds(pl.multiple_of(place, OWN), OWN), :] = ref[n * OWN : (n + 1) * OWN, :]


def fetch_kernel(scalars, coulomb, *refs):
    outs, sems = refs[:-1], refs[-1]
    copies = []
    for n, out in enumerate(outs):
        source = pl.ds(pl.multiple_of(scalars[n] * OWN, OWN), OWN)
        copies.append(pltpu.make_async_copy(coulomb.at[source, :], out, sems.at[n]))
        copies[-1].start()
    for copy in copies:
        copy.wait()


def block_kernel(left, right, tile, out, weighted):
    step = 512
    for t in range(0, right.shape[0], step):
        pair = pair_block(left[...], right[t : t + step, :]).astype(jnp.float32)
        weighted[:, t : t + step] = (
            pair * tile[:, t : t + step].astype(jnp.float32)
        ).astype(jnp.bfloat16)
    out[...] = jnp.dot(
        weighted[...], right[...], preferred_element_type=jnp.float32
    ).astype(out.dtype)


def block_sum(left, right, tile, dtype):
    columns = right.shape[0]
    return local(
        block_kernel,
        jax.ShapeDtypeStruct((OWN, NORB), dtype),
        left,
        right,
        tile,
        flops=4 * OWN * columns * NORB,
        scratch=[pltpu.VMEM((OWN, columns), jnp.bfloat16)],
    )


def local(kernel, out, *args, flops=0, far=None, scratch=()):
    def spec(n, a):
        if n == far:
            return hbm()
        return smem() if a.ndim == 1 else vmem()

    return pl.pallas_call(
        kernel,
        out_shape=out,
        in_specs=[spec(n, a) for n, a in enumerate(args)],
        out_specs=jax.tree.map(lambda _: vmem(), out),
        scratch_shapes=scratch,
        compiler_params=params(),
        cost_estimate=pl.CostEstimate(flops=flops, bytes_accessed=0, transcendentals=0),
    )(*args)


def select_kernel(others, per_owner, index, own, *refs):
    boxes = index.shape[0]
    spread = jnp.broadcast_to(index[...][:, None, :], (boxes, per_owner, LANES))
    diagonal = lax.broadcasted_iota(jnp.int32, spread.shape, 1) == lax.broadcasted_iota(
        jnp.int32, spread.shape, 2
    )
    picks = jnp.sum(jnp.where(diagonal, spread, 0).astype(jnp.float32), axis=2, keepdims=True)
    picks = picks.reshape(boxes * per_owner, 1).astype(jnp.int32)
    out = refs[-1]
    totals, rows = [], refs[0].shape[0]
    for n in range(OWN // rows):
        total = own[n * rows : (n + 1) * rows, :]
        for ref in refs[n * others : (n + 1) * others]:
            total = total + ref[...].astype(jnp.float32)
        totals.append(total.astype(jnp.bfloat16))
    projected = jnp.concatenate(totals)
    hot = picks == lax.broadcasted_iota(jnp.int32, (boxes * per_owner, OWN), 1)
    out[...] = jnp.dot(
        hot.astype(jnp.float32).astype(jnp.bfloat16), projected, preferred_element_type=jnp.float32
    ).astype(jnp.bfloat16)


def apply_kernel(interp, chosen, out, parts, sems):
    rows = parts.shape[1]
    copies = []
    for n in range(parts.shape[0]):
        parts[n] = -jnp.dot(
            interp[n * rows : (n + 1) * rows, :], chosen[...], preferred_element_type=jnp.float32
        )
        target = out.at[n * rows : (n + 1) * rows, :]
        copies.append(pltpu.make_async_copy(parts.at[n], target, sems.at[n]))
        copies[-1].start()
    for copy in copies:
        copy.wait()


def shards(orbitals, coulomb, interp, box_counts, owner_map, grid_rows, listed):
    row_count = lax.axis_size("row")
    col_count = lax.axis_size("col")
    box_total = row_count * col_count
    point_total = OWN * box_total
    capacity = (SLOTS + box_total - 1) // box_total
    per_owner = LIST // box_total
    my_row, my_col = lax.axis_index("row"), lax.axis_index("col")
    my_box = my_row * col_count + my_col
    packed = capacity * (NORB // LANES)
    packed = (packed // 8 + 1) * 8
    outgoing = pl.pallas_call(
        functools.partial(pick_kernel, box_total, capacity),
        out_shape=jax.ShapeDtypeStruct((box_total, packed, LANES), jnp.bfloat16),
        in_specs=[hbm()] * 5,
        out_specs=vmem(),
        scratch_shapes=[
            pltpu.SMEM((box_total,), jnp.int32),
            pltpu.VMEM((grid_rows.shape[1] // LANES, LANES), jnp.int32),
            pltpu.VMEM((point_total // LANES, LANES), jnp.int32),
            pltpu.VMEM((LIST // LANES, LANES), jnp.int32),
            pltpu.VMEM(orbitals.shape, jnp.bfloat16),
            pltpu.SemaphoreType.DMA((5,)),
        ],
        compiler_params=params(PICK_LIMIT),
        cost_estimate=pl.CostEstimate(
            flops=2 * SLOTS * LIST * NORB, bytes_accessed=2 << 20, transcendentals=0
        ),
    )(
        box_counts,
        grid_rows.reshape(grid_rows.shape[1] // LANES, LANES),
        owner_map.reshape(point_total // LANES, LANES),
        listed.reshape(LIST // LANES, LANES),
        orbitals,
    )
    received = lax.all_to_all(
        outgoing, ("row", "col"), split_axis=0, concat_axis=0, tiled=True
    )

    wanted_pos = my_box * OWN + jnp.arange(OWN, dtype=jnp.int32)
    all_listing = jnp.arange(point_total, dtype=jnp.int32)
    my_points = jnp.sum(
        jnp.where(owner_map[None, :] == wanted_pos[:, None], all_listing[None, :], 0), axis=1
    )
    box_ends = jnp.cumsum(box_counts)
    source = jnp.sum((my_points[:, None] >= box_ends[None, :]).astype(jnp.int32), axis=1)
    earlier = (source[:, None] == source[None, :]) & (my_points[None, :] < my_points[:, None])
    source_rank = jnp.sum(earlier.astype(jnp.int32), axis=1)
    index = (source * capacity + source_rank).reshape(OWN, 1)
    owned_rows, wanted = pl.pallas_call(
        functools.partial(place_kernel, capacity),
        out_shape=(
            jax.ShapeDtypeStruct((OWN, NORB), jnp.bfloat16),
            jax.ShapeDtypeStruct((box_total, LANES), jnp.int32),
        ),
        in_specs=[vmem(), vmem()],
        out_specs=(vmem(), vmem()),
        compiler_params=params(),
    )(index, received)

    def swap(rows, mask):
        return lax.ppermute(rows, "col", [(i, i ^ mask) for i in range(col_count)])

    def join(*rows):
        total = sum(r.shape[0] for r in rows)
        return local(join_kernel, jax.ShapeDtypeStruct((total, NORB), rows[0].dtype), *rows)

    def flip(rows, mask):
        return lax.ppermute(rows, "row", [(i, i ^ mask) for i in range(row_count)])

    left = {0: owned_rows}
    for mask in range(1, col_count):
        if mask & (mask - 1) == 0:
            left[mask] = swap(owned_rows, mask)

    whole = {0: owned_rows}
    half = OWN // 2
    single = [1 << b for b in range(1, row_count.bit_length() - 1)]
    double = [mask for mask in range(2, row_count, 2) if mask not in single]
    for mask in single:
        whole[mask] = flip(owned_rows, mask)
    passed_on = [owned_rows, join(*[whole[mask] for mask in single])]
    for mask in double:
        low, high = mask & -mask, 1 << (mask.bit_length() - 1)
        whole[mask] = join(
            flip(whole[mask ^ high][:half], high), flip(whole[mask ^ low][half:], low)
        )
    if double:
        passed_on.append(join(*[whole[mask] for mask in double]))
    masks = [0] + single + double
    shape = jax.ShapeDtypeStruct
    tiles = local(
        fetch_kernel,
        tuple(shape((OWN, row_count * OWN), jnp.bfloat16) for _ in range(col_count)),
        jnp.bitwise_xor(my_col, jnp.arange(col_count)).astype(jnp.int32),
        coulomb,
        far=1,
        scratch=[pltpu.SemaphoreType.DMA((col_count,))],
    )

    passed_on[-1], *tiles = lax.optimization_barrier((passed_on[-1], *tiles))
    mirrored = [flip(rows, 1) for rows in passed_on]
    direct = [mask for mask in left if mask]
    held = local(
        hold_kernel,
        tuple(shape(owned_rows.shape, owned_rows.dtype) for _ in direct),
        *[left[mask] for mask in direct],
        flops=20 * 10**9,
    )
    *held, mirrored[-1] = lax.optimization_barrier((*held, mirrored[-1]))
    left.update(zip(direct, held))
    for mask in range(1, col_count):
        if mask not in left:
            low = mask & -mask
            left[mask] = swap(left[mask ^ low], low)

    right = local(
        functools.partial(order_kernel, masks),
        shape((row_count * OWN, NORB), jnp.bfloat16),
        my_row.reshape(1).astype(jnp.int32),
        *passed_on,
        *mirrored,
    )
    def partial_sum(mask, dtype):
        return block_sum(left[mask], right, tiles[mask], dtype)

    arrived = []
    for mask in sorted(range(1, col_count), key=lambda m: (m & 1, m)):
        arrived.append(swap(partial_sum(mask, jnp.bfloat16), mask))
    own_sum = partial_sum(0, jnp.float32)
    picked = pl.pallas_call(
        functools.partial(select_kernel, col_count - 1, per_owner),
        out_shape=jax.ShapeDtypeStruct((LIST, NORB), jnp.bfloat16),
        in_specs=[vmem()] * (2 + len(arrived)),
        out_specs=vmem(),
        compiler_params=params(),
    )(wanted, own_sum, *arrived)
    chosen = lax.all_to_all(
        picked.reshape(box_total, per_owner, NORB),
        ("row", "col"),
        split_axis=0,
        concat_axis=0,
        tiled=True,
    ).reshape(LIST, NORB)
    box, count = interp.shape[0], 4
    return pl.pallas_call(
        apply_kernel,
        out_shape=jax.ShapeDtypeStruct((box, NORB), jnp.float32),
        in_specs=[vmem(), vmem()],
        out_specs=hbm(),
        scratch_shapes=[
            pltpu.VMEM((count, box // count, NORB), jnp.float32),
            pltpu.SemaphoreType.DMA((count,)),
        ],
        compiler_params=params(),
    )(interp, chosen)


def solution(mesh):
    return jax.shard_map(
        shards,
        mesh=mesh,
        in_specs=(
            P(("row", "col"), None),
            P("row", "col"),
            P(("row", "col"), None),
            P(),
            P(),
            P(("row", "col"), None),
            P(("row", "col"), None),
        ),
        out_specs=P(("row", "col"), None),
        check_vma=False,
    )
```

```python
import functools

import jax
import jax.numpy as jnp
from jax import lax
from jax.experimental import pallas as pl
from jax.experimental.pallas import tpu as pltpu
from jax.sharding import PartitionSpec as P

NORB = 512
LIST = 1024
OWN = 256
SLOTS = 768
LANES = 128
UPPER = 160
VMEM_LIMIT = 48 * 1024 * 1024
PICK_LIMIT = 60 * 1024 * 1024


def vmem():
    return pl.BlockSpec(memory_space=pltpu.VMEM)


def smem():
    return pl.BlockSpec(memory_space=pltpu.SMEM)


def hbm():
    return pl.BlockSpec(memory_space=pltpu.HBM)


def params(limit=VMEM_LIMIT):
    return pltpu.CompilerParams(vmem_limit_bytes=limit)


def pick_kernel(
    box_total, capacity, counts_hbm, grid_hbm, owner_hbm, listed_hbm, orbitals_hbm, out,
    counts, grid_rows, owner_map, listed, orbitals, sems,
):
    copies = [
        pltpu.make_async_copy(source, target, sems.at[n])
        for n, (source, target) in enumerate(
            [
                (counts_hbm, counts),
                (grid_hbm, grid_rows),
                (owner_hbm, owner_map),
                (listed_hbm, listed),
                (orbitals_hbm, orbitals),
            ]
        )
    ]
    for copy in copies:
        copy.start()
    targets = box_total * capacity
    my_box = lax.axis_index("row") * lax.axis_size("col") + lax.axis_index("col")
    copies[0].wait()
    start = jnp.int32(0)
    for b in range(box_total):
        start = start + jnp.where(b < my_box, counts[b], 0)
    stop = start + counts[my_box]
    first = start // LANES
    shift = start - first * LANES
    blocks = SLOTS // LANES + 1
    top = owner_map.shape[0] - 1
    lane = lax.broadcasted_iota(jnp.int32, (1, LANES), 1)
    copies[1].wait()
    copies[2].wait()
    turned = pltpu.roll(grid_rows[...], shift, 1)
    lane8 = lax.broadcasted_iota(jnp.int32, turned.shape, 1)
    lined = jnp.where(lane8 < shift, pltpu.roll(turned, 1, 0), turned)
    before = (
        lax.broadcasted_iota(jnp.int32, (LANES, LANES), 0)
        < lax.broadcasted_iota(jnp.int32, (LANES, LANES), 1)
    ).astype(jnp.bfloat16)
    owner_ids = lax.broadcasted_iota(jnp.int32, (box_total, LANES), 0)
    target_ids = lax.broadcasted_iota(jnp.int32, (targets, LANES), 0)
    base = jnp.zeros((box_total, 1), jnp.float32)
    found = jnp.zeros((targets, LANES), jnp.int32)
    for i in range(blocks):
        k = (first + i) * LANES + lane
        position = owner_map[pl.ds(jnp.minimum(first + i, top), 1), :]
        live = (k >= start) & (k < stop)
        owner = jnp.where(live, position // OWN, -1)
        member = (owner_ids == owner).astype(jnp.float32)
        inner = jnp.dot(member.astype(jnp.bfloat16), before, preferred_element_type=jnp.float32)
        rank = jnp.sum(member * (inner + base), axis=0, keepdims=True).astype(jnp.int32)
        base = base + jnp.sum(member, axis=1, keepdims=True)
        target = jnp.where(live, owner * capacity + rank, -1)
        found = found + jnp.where(target_ids == target, lined[i : i + 1, :] + 1, 0)
    source = jnp.sum(found.astype(jnp.float32), axis=1, keepdims=True).astype(jnp.int32) - 1
    copies[3].wait()
    per_owner = LIST // box_total
    fold = LANES // per_owner
    spread = jnp.broadcast_to(listed[...][:, None, :], (LIST // LANES, fold, LANES))
    spread = spread.reshape(box_total, LANES)
    phase = lax.broadcasted_iota(jnp.int32, spread.shape, 0) % fold
    indices = spread
    for q in range(1, fold):
        indices = jnp.where(phase == q, pltpu.roll(spread, LANES - q * per_owner, 1), indices)
    indices = indices.astype(jnp.float32).astype(jnp.bfloat16)
    tail = out.shape[1] - capacity * (NORB // LANES)
    out[:, capacity * (NORB // LANES) :, :] = jnp.broadcast_to(
        indices[:, None, :], (box_total, tail, LANES)
    )
    box = orbitals.shape[0]
    step = targets // 4
    copies[4].wait()
    for t in range(0, targets, step):
        hot = source[t : t + step] == lax.broadcasted_iota(jnp.int32, (step, box), 1)
        rows = jnp.dot(
            hot.astype(jnp.float32).astype(jnp.bfloat16),
            orbitals[...],
            preferred_element_type=jnp.float32,
        ).astype(jnp.bfloat16)
        first_owner = t // capacity
        for c in range(NORB // LANES):
            out[
                first_owner : first_owner + step // capacity, c * capacity : (c + 1) * capacity, :
            ] = rows[:, c * LANES : (c + 1) * LANES].reshape(step // capacity, capacity, LANES)


def place_kernel(capacity, index, received, out, wanted):
    boxes = received.shape[0]
    rows = jnp.concatenate(
        [
            received[:, c * capacity : (c + 1) * capacity, :].reshape(boxes * capacity, LANES)
            for c in range(NORB // LANES)
        ],
        axis=1,
    )
    hot = index[...] == lax.broadcasted_iota(jnp.int32, (index.shape[0], rows.shape[0]), 1)
    out[...] = jnp.dot(
        hot.astype(jnp.float32).astype(jnp.bfloat16), rows, preferred_element_type=jnp.float32
    ).astype(jnp.bfloat16)
    tail = received[:, capacity * (NORB // LANES) :, :].astype(jnp.float32)
    wanted[...] = tail[:, 0, :].astype(jnp.int32)


def join_kernel(*refs):
    out, at = refs[-1], 0
    for ref in refs[:-1]:
        out[at : at + ref.shape[0], :] = ref[...]
        at += ref.shape[0]


def hold_kernel(*refs):
    count = len(refs) // 2
    for source, target in zip(refs[:count], refs[count:]):
        target[...] = source[...]


def pair_block(left, right):
    return lax.dot_general(
        left, right, (((1,), (1,)), ((), ())), preferred_element_type=jnp.float32
    ).astype(jnp.bfloat16)


def order_kernel(masks, scalars, *refs):
    pieces, out = refs[:-1], refs[-1]
    places = [mask ^ parity for parity in (0, 1) for mask in masks]
    for ref in pieces:
        for n in range(ref.shape[0] // OWN):
            place = jnp.bitwise_xor(scalars[0], places.pop(0)) * OWN
            out[pl.ds(pl.multiple_of(place, OWN), OWN), :] = ref[n * OWN : (n + 1) * OWN, :]


def fetch_kernel(scalars, coulomb, *refs):
    outs, sems = refs[:-1], refs[-1]
    copies = []
    for n, out in enumerate(outs):
        source = pl.ds(pl.multiple_of(scalars[n] * OWN, OWN), OWN)
        copies.append(pltpu.make_async_copy(coulomb.at[source, :], out, sems.at[n]))
        copies[-1].start()
    for copy in copies:
        copy.wait()


def block_kernel(count, left, right, tile, *refs):
    earlier, outs, weighted = refs[: -1 - count], refs[-1 - count : -1], refs[-1]
    step = 512
    for t in range(0, right.shape[0], step):
        pair = pair_block(left[...], right[t : t + step, :]).astype(jnp.float32)
        weighted[:, t : t + step] = (
            pair * tile[:, t : t + step].astype(jnp.float32)
        ).astype(jnp.bfloat16)
    total = jnp.dot(weighted[...], right[...], preferred_element_type=jnp.float32)
    at = 0
    for out in outs:
        rows = out.shape[0]
        out[...] = total[at : at + rows, :].astype(out.dtype)
        at += rows
    for ref in earlier:
        rows = ref.shape[0]
        outs[0][:rows, :] = total[:rows, :] + ref[...].astype(jnp.float32)


def add_kernel(one, other, out):
    out[...] = (one[...] + other[...].astype(jnp.float32)).astype(out.dtype)


def block_sum(left, right, tile, *parts, earlier=(), flops=0):
    return local(
        functools.partial(block_kernel, len(parts)),
        tuple(jax.ShapeDtypeStruct((rows, NORB), dtype) for rows, dtype in parts),
        left,
        right,
        tile,
        *earlier,
        flops=flops,
        scratch=[pltpu.VMEM((OWN, right.shape[0]), jnp.bfloat16)],
    )


def local(kernel, out, *args, flops=0, far=None, scratch=()):
    def spec(n, a):
        if n == far:
            return hbm()
        return smem() if a.ndim == 1 else vmem()

    return pl.pallas_call(
        kernel,
        out_shape=out,
        in_specs=[spec(n, a) for n, a in enumerate(args)],
        out_specs=jax.tree.map(lambda _: vmem(), out),
        scratch_shapes=scratch,
        compiler_params=params(),
        cost_estimate=pl.CostEstimate(flops=flops, bytes_accessed=0, transcendentals=0),
    )(*args)


def select_kernel(per_owner, index, own, *refs):
    boxes = index.shape[0]
    spread = jnp.broadcast_to(index[...][:, None, :], (boxes, per_owner, LANES))
    diagonal = lax.broadcasted_iota(jnp.int32, spread.shape, 1) == lax.broadcasted_iota(
        jnp.int32, spread.shape, 2
    )
    picks = jnp.sum(jnp.where(diagonal, spread, 0).astype(jnp.float32), axis=2, keepdims=True)
    picks = picks.reshape(boxes * per_owner, 1).astype(jnp.int32)
    out = refs[-1]
    totals = []
    for rows in (slice(0, UPPER), slice(UPPER, OWN)):
        total = own[rows, :]
        for ref in refs[:-1]:
            if ref.shape[0] == OWN:
                total = total + ref[rows, :].astype(jnp.float32)
            elif ref.shape[0] == rows.stop - rows.start:
                total = total + ref[...].astype(jnp.float32)
        totals.append(total.astype(jnp.bfloat16))
    projected = jnp.concatenate(totals)
    hot = picks == lax.broadcasted_iota(jnp.int32, (boxes * per_owner, OWN), 1)
    out[...] = jnp.dot(
        hot.astype(jnp.float32).astype(jnp.bfloat16), projected, preferred_element_type=jnp.float32
    ).astype(jnp.bfloat16)


def apply_kernel(interp, chosen, out, parts, sems):
    rows = parts.shape[1]
    copies = []
    for n in range(parts.shape[0]):
        parts[n] = -jnp.dot(
            interp[n * rows : (n + 1) * rows, :], chosen[...], preferred_element_type=jnp.float32
        )
        target = out.at[n * rows : (n + 1) * rows, :]
        copies.append(pltpu.make_async_copy(parts.at[n], target, sems.at[n]))
        copies[-1].start()
    for copy in copies:
        copy.wait()


def shards(orbitals, coulomb, interp, box_counts, owner_map, grid_rows, listed):
    row_count = lax.axis_size("row")
    col_count = lax.axis_size("col")
    box_total = row_count * col_count
    point_total = OWN * box_total
    capacity = (SLOTS + box_total - 1) // box_total
    per_owner = LIST // box_total
    my_row, my_col = lax.axis_index("row"), lax.axis_index("col")
    my_box = my_row * col_count + my_col
    packed = capacity * (NORB // LANES)
    packed = (packed // 8 + 1) * 8
    outgoing = pl.pallas_call(
        functools.partial(pick_kernel, box_total, capacity),
        out_shape=jax.ShapeDtypeStruct((box_total, packed, LANES), jnp.bfloat16),
        in_specs=[hbm()] * 5,
        out_specs=vmem(),
        scratch_shapes=[
            pltpu.SMEM((box_total,), jnp.int32),
            pltpu.VMEM((grid_rows.shape[1] // LANES, LANES), jnp.int32),
            pltpu.VMEM((point_total // LANES, LANES), jnp.int32),
            pltpu.VMEM((LIST // LANES, LANES), jnp.int32),
            pltpu.VMEM(orbitals.shape, jnp.bfloat16),
            pltpu.SemaphoreType.DMA((5,)),
        ],
        compiler_params=params(PICK_LIMIT),
        cost_estimate=pl.CostEstimate(
            flops=2 * SLOTS * LIST * NORB, bytes_accessed=2 << 20, transcendentals=0
        ),
    )(
        box_counts,
        grid_rows.reshape(grid_rows.shape[1] // LANES, LANES),
        owner_map.reshape(point_total // LANES, LANES),
        listed.reshape(LIST // LANES, LANES),
        orbitals,
    )
    received = lax.all_to_all(
        outgoing, ("row", "col"), split_axis=0, concat_axis=0, tiled=True
    )

    wanted_pos = my_box * OWN + jnp.arange(OWN, dtype=jnp.int32)
    all_listing = jnp.arange(point_total, dtype=jnp.int32)
    my_points = jnp.sum(
        jnp.where(owner_map[None, :] == wanted_pos[:, None], all_listing[None, :], 0), axis=1
    )
    box_ends = jnp.cumsum(box_counts)
    source = jnp.sum((my_points[:, None] >= box_ends[None, :]).astype(jnp.int32), axis=1)
    earlier = (source[:, None] == source[None, :]) & (my_points[None, :] < my_points[:, None])
    source_rank = jnp.sum(earlier.astype(jnp.int32), axis=1)
    index = (source * capacity + source_rank).reshape(OWN, 1)
    owned_rows, wanted = pl.pallas_call(
        functools.partial(place_kernel, capacity),
        out_shape=(
            jax.ShapeDtypeStruct((OWN, NORB), jnp.bfloat16),
            jax.ShapeDtypeStruct((box_total, LANES), jnp.int32),
        ),
        in_specs=[vmem(), vmem()],
        out_specs=(vmem(), vmem()),
        compiler_params=params(),
    )(index, received)

    def swap(rows, mask):
        return lax.ppermute(rows, "col", [(i, i ^ mask) for i in range(col_count)])

    def join(*rows):
        total = sum(r.shape[0] for r in rows)
        return local(join_kernel, jax.ShapeDtypeStruct((total, NORB), rows[0].dtype), *rows)

    def flip(rows, mask):
        return lax.ppermute(rows, "row", [(i, i ^ mask) for i in range(row_count)])

    left = {0: owned_rows}
    for mask in range(1, col_count):
        if mask & (mask - 1) == 0:
            left[mask] = swap(owned_rows, mask)

    whole = {0: owned_rows}
    half = OWN // 2
    single = [1 << b for b in range(1, row_count.bit_length() - 1)]
    double = [mask for mask in range(2, row_count, 2) if mask not in single]
    for mask in single:
        whole[mask] = flip(owned_rows, mask)
    passed_on = [owned_rows, join(*[whole[mask] for mask in single])]
    for mask in double:
        low, high = mask & -mask, 1 << (mask.bit_length() - 1)
        whole[mask] = join(
            flip(whole[mask ^ high][:half], high), flip(whole[mask ^ low][half:], low)
        )
    if double:
        passed_on.append(join(*[whole[mask] for mask in double]))
    masks = [0] + single + double
    shape = jax.ShapeDtypeStruct
    tiles = local(
        fetch_kernel,
        tuple(shape((OWN, row_count * OWN), jnp.bfloat16) for _ in range(col_count)),
        jnp.bitwise_xor(my_col, jnp.arange(col_count)).astype(jnp.int32),
        coulomb,
        far=1,
        scratch=[pltpu.SemaphoreType.DMA((col_count,))],
    )

    passed_on[-1], *tiles = lax.optimization_barrier((passed_on[-1], *tiles))
    mirrored = [flip(rows, 1) for rows in passed_on]
    direct = [mask for mask in left if mask]
    held = local(
        hold_kernel,
        tuple(shape(owned_rows.shape, owned_rows.dtype) for _ in direct),
        *[left[mask] for mask in direct],
        flops=20 * 10**9,
    )
    *held, mirrored[0] = lax.optimization_barrier((*held, mirrored[0]))
    left.update(zip(direct, held))
    for mask in range(1, col_count):
        if mask not in left:
            low = mask & -mask
            left[mask] = swap(left[mask ^ low], low)

    right = local(
        functools.partial(order_kernel, masks),
        shape((row_count * OWN, NORB), jnp.bfloat16),
        my_row.reshape(1).astype(jnp.int32),
        *passed_on,
        *mirrored,
    )
    def partial_sum(mask, *parts, **options):
        return block_sum(left[mask], right, tiles[mask], *parts, **options)

    short, wide = jnp.bfloat16, jnp.float32
    upper_two, lower_two = partial_sum(2, (UPPER, short), (OWN - UPPER, wide))
    left[3], _ = lax.optimization_barrier((left[3], upper_two))
    upper_three, lower_three = partial_sum(3, (UPPER, short), (OWN - UPPER, short))
    first = swap(upper_two, 2)
    handed = swap(lower_three, 1)
    arrived = [swap(upper_three, 3)]
    lower = local(add_kernel, shape(lower_two.shape, short), lower_two, handed)
    arrived.append(swap(lower, 2))
    left[1], _ = lax.optimization_barrier((left[1], upper_three))
    for mask in [1, *range(4, col_count)]:
        arrived.append(swap(partial_sum(mask, (OWN, short))[0], mask))
    (own_sum,) = partial_sum(0, (OWN, wide), earlier=[first], flops=10**10)
    picked = pl.pallas_call(
        functools.partial(select_kernel, per_owner),
        out_shape=jax.ShapeDtypeStruct((LIST, NORB), jnp.bfloat16),
        in_specs=[vmem()] * (2 + len(arrived)),
        out_specs=vmem(),
        compiler_params=params(),
    )(wanted, own_sum, *arrived)
    chosen = lax.all_to_all(
        picked.reshape(box_total, per_owner, NORB),
        ("row", "col"),
        split_axis=0,
        concat_axis=0,
        tiled=True,
    ).reshape(LIST, NORB)
    box, count = interp.shape[0], 4
    return pl.pallas_call(
        apply_kernel,
        out_shape=jax.ShapeDtypeStruct((box, NORB), jnp.float32),
        in_specs=[vmem(), vmem()],
        out_specs=hbm(),
        scratch_shapes=[
            pltpu.VMEM((count, box // count, NORB), jnp.float32),
            pltpu.SemaphoreType.DMA((count,)),
        ],
        compiler_params=params(),
    )(interp, chosen)


def solution(mesh):
    return jax.shard_map(
        shards,
        mesh=mesh,
        in_specs=(
            P(("row", "col"), None),
            P("row", "col"),
            P(("row", "col"), None),
            P(),
            P(),
            P(("row", "col"), None),
            P(("row", "col"), None),
        ),
        out_specs=P(("row", "col"), None),
        check_vma=False,
    )
```

```python
import functools

import jax
import jax.numpy as jnp
from jax import lax
from jax.experimental import pallas as pl
from jax.experimental.pallas import tpu as pltpu
from jax.sharding import PartitionSpec as P

NORB = 512
LIST = 1024
OWN = 256
SLOTS = 768
LANES = 128
CUT = 96
VMEM_LIMIT = 48 * 1024 * 1024
PICK_LIMIT = 60 * 1024 * 1024


def vmem():
    return pl.BlockSpec(memory_space=pltpu.VMEM)


def smem():
    return pl.BlockSpec(memory_space=pltpu.SMEM)


def hbm():
    return pl.BlockSpec(memory_space=pltpu.HBM)


def params(limit=VMEM_LIMIT):
    return pltpu.CompilerParams(vmem_limit_bytes=limit)


def pick_kernel(
    box_total, capacity, counts_hbm, grid_hbm, owner_hbm, listed_hbm, orbitals_hbm, out,
    counts, grid_rows, owner_map, listed, orbitals, sems,
):
    copies = [
        pltpu.make_async_copy(source, target, sems.at[n])
        for n, (source, target) in enumerate(
            [
                (counts_hbm, counts),
                (grid_hbm, grid_rows),
                (owner_hbm, owner_map),
                (listed_hbm, listed),
                (orbitals_hbm, orbitals),
            ]
        )
    ]
    for copy in copies:
        copy.start()
    targets = box_total * capacity
    my_box = lax.axis_index("row") * lax.axis_size("col") + lax.axis_index("col")
    copies[0].wait()
    start = jnp.int32(0)
    for b in range(box_total):
        start = start + jnp.where(b < my_box, counts[b], 0)
    stop = start + counts[my_box]
    first = start // LANES
    shift = start - first * LANES
    blocks = SLOTS // LANES + 1
    top = owner_map.shape[0] - 1
    lane = lax.broadcasted_iota(jnp.int32, (1, LANES), 1)
    copies[1].wait()
    copies[2].wait()
    turned = pltpu.roll(grid_rows[...], shift, 1)
    lane8 = lax.broadcasted_iota(jnp.int32, turned.shape, 1)
    lined = jnp.where(lane8 < shift, pltpu.roll(turned, 1, 0), turned)
    before = (
        lax.broadcasted_iota(jnp.int32, (LANES, LANES), 0)
        < lax.broadcasted_iota(jnp.int32, (LANES, LANES), 1)
    ).astype(jnp.bfloat16)
    owner_ids = lax.broadcasted_iota(jnp.int32, (box_total, LANES), 0)
    target_ids = lax.broadcasted_iota(jnp.int32, (targets, LANES), 0)
    base = jnp.zeros((box_total, 1), jnp.float32)
    found = jnp.zeros((targets, LANES), jnp.int32)
    for i in range(blocks):
        k = (first + i) * LANES + lane
        position = owner_map[pl.ds(jnp.minimum(first + i, top), 1), :]
        live = (k >= start) & (k < stop)
        owner = jnp.where(live, position // OWN, -1)
        member = (owner_ids == owner).astype(jnp.float32)
        inner = jnp.dot(member.astype(jnp.bfloat16), before, preferred_element_type=jnp.float32)
        rank = jnp.sum(member * (inner + base), axis=0, keepdims=True).astype(jnp.int32)
        base = base + jnp.sum(member, axis=1, keepdims=True)
        target = jnp.where(live, owner * capacity + rank, -1)
        found = found + jnp.where(target_ids == target, lined[i : i + 1, :] + 1, 0)
    source = jnp.sum(found.astype(jnp.float32), axis=1, keepdims=True).astype(jnp.int32) - 1
    copies[3].wait()
    per_owner = LIST // box_total
    fold = LANES // per_owner
    spread = jnp.broadcast_to(listed[...][:, None, :], (LIST // LANES, fold, LANES))
    spread = spread.reshape(box_total, LANES)
    phase = lax.broadcasted_iota(jnp.int32, spread.shape, 0) % fold
    indices = spread
    for q in range(1, fold):
        indices = jnp.where(phase == q, pltpu.roll(spread, LANES - q * per_owner, 1), indices)
    indices = indices.astype(jnp.float32).astype(jnp.bfloat16)
    tail = out.shape[1] - capacity * (NORB // LANES)
    out[:, capacity * (NORB // LANES) :, :] = jnp.broadcast_to(
        indices[:, None, :], (box_total, tail, LANES)
    )
    box = orbitals.shape[0]
    step = targets // 4
    copies[4].wait()
    for t in range(0, targets, step):
        hot = source[t : t + step] == lax.broadcasted_iota(jnp.int32, (step, box), 1)
        rows = jnp.dot(
            hot.astype(jnp.float32).astype(jnp.bfloat16),
            orbitals[...],
            preferred_element_type=jnp.float32,
        )
        owners = step // capacity
        packed = jnp.concatenate(
            [
                rows[:, c : c + LANES].reshape(owners, capacity, LANES)
                for c in range(0, NORB, LANES)
            ],
            axis=1,
        )
        first_owner = t // capacity
        out[first_owner : first_owner + owners, : packed.shape[1], :] = packed.astype(jnp.bfloat16)


def place_kernel(capacity, index, received, out, wanted):
    boxes = received.shape[0]
    packed = received[:, : capacity * (NORB // LANES), :].astype(jnp.float32)
    rows = jnp.concatenate(
        [
            packed[:, c * capacity : (c + 1) * capacity, :].reshape(boxes * capacity, LANES)
            for c in range(NORB // LANES)
        ],
        axis=1,
    ).astype(jnp.bfloat16)
    hot = index[...] == lax.broadcasted_iota(jnp.int32, (index.shape[0], rows.shape[0]), 1)
    out[...] = jnp.dot(
        hot.astype(jnp.float32).astype(jnp.bfloat16), rows, preferred_element_type=jnp.float32
    ).astype(jnp.bfloat16)
    tail = received[:, capacity * (NORB // LANES) :, :].astype(jnp.float32)
    wanted[...] = tail[:, 0, :].astype(jnp.int32)


def join_kernel(*refs):
    out, at = refs[-1], 0
    for ref in refs[:-1]:
        out[at : at + ref.shape[0], :] = ref[...]
        at += ref.shape[0]


def hold_kernel(*refs):
    count = len(refs) // 2
    for source, target in zip(refs[:count], refs[count:]):
        target[...] = source[...]


def pair_block(left, right):
    return lax.dot_general(
        left, right, (((1,), (1,)), ((), ())), preferred_element_type=jnp.float32
    ).astype(jnp.bfloat16)


def order_kernel(masks, scalars, *refs):
    pieces, out = refs[:-1], refs[-1]
    places = [mask ^ parity for parity in (0, 1) for mask in masks]
    for ref in pieces:
        for n in range(ref.shape[0] // OWN):
            place = jnp.bitwise_xor(scalars[0], places.pop(0)) * OWN
            out[pl.ds(pl.multiple_of(place, OWN), OWN), :] = ref[n * OWN : (n + 1) * OWN, :]


def fetch_kernel(scalars, coulomb, *refs):
    outs, sems = refs[:-1], refs[-1]
    copies = []
    for n, out in enumerate(outs):
        source = pl.ds(pl.multiple_of(scalars[n] * OWN, OWN), OWN)
        copies.append(pltpu.make_async_copy(coulomb.at[source, :], out, sems.at[n]))
        copies[-1].start()
    for copy in copies:
        copy.wait()


def block_kernel(count, spans, at, *refs):
    lefts, right, tile = refs[:count], refs[count], refs[count + 1]
    earlier, outs, weighted = refs[count + 2 : -1 - len(spans)], refs[-1 - len(spans) : -1], refs[-1]
    left = jnp.concatenate([ref[...] for ref in lefts]) if count > 1 else lefts[0][...]
    rows = slice(at, at + left.shape[0])
    step = 512
    for t in range(0, right.shape[0], step):
        pair = pair_block(left, right[t : t + step, :]).astype(jnp.float32)
        weighted[:, t : t + step] = (
            pair * tile[rows, t : t + step].astype(jnp.float32)
        ).astype(jnp.bfloat16)
    total = jnp.dot(weighted[...], right[...], preferred_element_type=jnp.float32)
    for out, (low, high) in zip(outs, spans):
        out[...] = total[low:high, :].astype(out.dtype)
    for ref in earlier:
        low = total.shape[0] - ref.shape[0]
        outs[0][low:, :] = total[low:, :] + ref[...].astype(jnp.float32)


def add_kernel(one, other, out):
    out[...] = (one[...] + other[...].astype(jnp.float32)).astype(out.dtype)


def block_sum(lefts, right, tile, *parts, at=0, earlier=(), flops=0):
    spans, low = [], 0
    for rows, _ in parts:
        spans.append((low, low + rows))
        low += rows
    return local(
        functools.partial(block_kernel, len(lefts), spans, at),
        tuple(jax.ShapeDtypeStruct((rows, NORB), dtype) for rows, dtype in parts),
        *lefts,
        right,
        tile,
        *earlier,
        flops=flops,
        scratch=[pltpu.VMEM((low, right.shape[0]), jnp.bfloat16)],
    )


def local(kernel, out, *args, flops=0, far=None, scratch=()):
    def spec(n, a):
        if n == far:
            return hbm()
        return smem() if a.ndim == 1 else vmem()

    return pl.pallas_call(
        kernel,
        out_shape=out,
        in_specs=[spec(n, a) for n, a in enumerate(args)],
        out_specs=jax.tree.map(lambda _: vmem(), out),
        scratch_shapes=scratch,
        compiler_params=params(),
        cost_estimate=pl.CostEstimate(flops=flops, bytes_accessed=0, transcendentals=0),
    )(*args)


def select_kernel(per_owner, firsts, index, own, *refs):
    boxes = index.shape[0]
    spread = jnp.broadcast_to(index[...][:, None, :], (boxes, per_owner, LANES))
    diagonal = lax.broadcasted_iota(jnp.int32, spread.shape, 1) == lax.broadcasted_iota(
        jnp.int32, spread.shape, 2
    )
    picks = jnp.sum(jnp.where(diagonal, spread, 0).astype(jnp.float32), axis=2, keepdims=True)
    picks = picks.reshape(boxes * per_owner, 1).astype(jnp.int32)
    out = refs[-1]
    totals = []
    for low, high in ((0, CUT), (CUT, OWN)):
        total = own[low:high, :]
        for ref, first in zip(refs[:-1], firsts):
            if first <= low < first + ref.shape[0]:
                total = total + ref[low - first : high - first, :].astype(jnp.float32)
        totals.append(total.astype(jnp.bfloat16))
    projected = jnp.concatenate(totals)
    hot = picks == lax.broadcasted_iota(jnp.int32, (boxes * per_owner, OWN), 1)
    out[...] = jnp.dot(
        hot.astype(jnp.float32).astype(jnp.bfloat16), projected, preferred_element_type=jnp.float32
    ).astype(jnp.bfloat16)


def apply_kernel(interp, chosen, out, parts, sems):
    rows = parts.shape[1]
    copies = []
    for n in range(parts.shape[0]):
        parts[n] = -jnp.dot(
            interp[n * rows : (n + 1) * rows, :], chosen[...], preferred_element_type=jnp.float32
        )
        target = out.at[n * rows : (n + 1) * rows, :]
        copies.append(pltpu.make_async_copy(parts.at[n], target, sems.at[n]))
        copies[-1].start()
    for copy in copies:
        copy.wait()


def shards(orbitals, coulomb, interp, box_counts, owner_map, grid_rows, listed):
    row_count = lax.axis_size("row")
    col_count = lax.axis_size("col")
    box_total = row_count * col_count
    point_total = OWN * box_total
    capacity = (SLOTS + box_total - 1) // box_total
    per_owner = LIST // box_total
    my_row, my_col = lax.axis_index("row"), lax.axis_index("col")
    my_box = my_row * col_count + my_col
    packed = capacity * (NORB // LANES)
    packed = (packed // 8 + 1) * 8
    outgoing = pl.pallas_call(
        functools.partial(pick_kernel, box_total, capacity),
        out_shape=jax.ShapeDtypeStruct((box_total, packed, LANES), jnp.bfloat16),
        in_specs=[hbm()] * 5,
        out_specs=vmem(),
        scratch_shapes=[
            pltpu.SMEM((box_total,), jnp.int32),
            pltpu.VMEM((grid_rows.shape[1] // LANES, LANES), jnp.int32),
            pltpu.VMEM((point_total // LANES, LANES), jnp.int32),
            pltpu.VMEM((LIST // LANES, LANES), jnp.int32),
            pltpu.VMEM(orbitals.shape, jnp.bfloat16),
            pltpu.SemaphoreType.DMA((5,)),
        ],
        compiler_params=params(PICK_LIMIT),
        cost_estimate=pl.CostEstimate(
            flops=2 * SLOTS * LIST * NORB, bytes_accessed=2 << 20, transcendentals=0
        ),
    )(
        box_counts,
        grid_rows.reshape(grid_rows.shape[1] // LANES, LANES),
        owner_map.reshape(point_total // LANES, LANES),
        listed.reshape(LIST // LANES, LANES),
        orbitals,
    )
    received = lax.all_to_all(
        outgoing, ("row", "col"), split_axis=0, concat_axis=0, tiled=True
    )

    wanted_pos = my_box * OWN + jnp.arange(OWN, dtype=jnp.int32)
    all_listing = jnp.arange(point_total, dtype=jnp.int32)
    my_points = jnp.sum(
        jnp.where(owner_map[None, :] == wanted_pos[:, None], all_listing[None, :], 0), axis=1
    )
    box_ends = jnp.cumsum(box_counts)
    source = jnp.sum((my_points[:, None] >= box_ends[None, :]).astype(jnp.int32), axis=1)
    earlier = (source[:, None] == source[None, :]) & (my_points[None, :] < my_points[:, None])
    source_rank = jnp.sum(earlier.astype(jnp.int32), axis=1)
    index = (source * capacity + source_rank).reshape(OWN, 1)
    owned_rows, wanted = pl.pallas_call(
        functools.partial(place_kernel, capacity),
        out_shape=(
            jax.ShapeDtypeStruct((OWN, NORB), jnp.bfloat16),
            jax.ShapeDtypeStruct((box_total, LANES), jnp.int32),
        ),
        in_specs=[vmem(), vmem()],
        out_specs=(vmem(), vmem()),
        compiler_params=params(),
    )(index, received)

    def swap(rows, mask):
        return lax.ppermute(rows, "col", [(i, i ^ mask) for i in range(col_count)])

    def join(*rows):
        total = sum(r.shape[0] for r in rows)
        return local(join_kernel, jax.ShapeDtypeStruct((total, NORB), rows[0].dtype), *rows)

    def flip(rows, mask):
        return lax.ppermute(rows, "row", [(i, i ^ mask) for i in range(row_count)])

    half = OWN // 2
    left = {0: [owned_rows]}
    for mask in range(1, col_count):
        if mask & (mask - 1) == 0:
            left[mask] = [swap(owned_rows, mask)]

    whole = {0: owned_rows}
    single = [1 << b for b in range(1, row_count.bit_length() - 1)]
    double = [mask for mask in range(2, row_count, 2) if mask not in single]
    for mask in single:
        whole[mask] = flip(owned_rows, mask)
    passed_on = [owned_rows, join(*[whole[mask] for mask in single])]
    for mask in double:
        low, high = mask & -mask, 1 << (mask.bit_length() - 1)
        whole[mask] = join(
            flip(whole[mask ^ high][:half], high), flip(whole[mask ^ low][half:], low)
        )
    if double:
        passed_on.append(join(*[whole[mask] for mask in double]))
    masks = [0] + single + double
    shape = jax.ShapeDtypeStruct
    tiles = local(
        fetch_kernel,
        tuple(shape((OWN, row_count * OWN), jnp.bfloat16) for _ in range(col_count)),
        jnp.bitwise_xor(my_col, jnp.arange(col_count)).astype(jnp.int32),
        coulomb,
        far=1,
        scratch=[pltpu.SemaphoreType.DMA((col_count,))],
    )

    passed_on[-1], *tiles = lax.optimization_barrier((passed_on[-1], *tiles))
    mirrored = [flip(rows, 1) for rows in passed_on]
    direct = [mask for mask in left if mask]
    held = local(
        hold_kernel,
        tuple(shape(owned_rows.shape, owned_rows.dtype) for _ in direct),
        *[left[mask][0] for mask in direct],
        flops=20 * 10**9,
    )
    *held, mirrored[0] = lax.optimization_barrier((*held, mirrored[0]))
    left.update((mask, [rows]) for mask, rows in zip(direct, held))
    for mask in range(3, col_count):
        if mask not in left:
            low = mask & -mask
            (rows,) = left[mask ^ low]
            parts = [rows[:CUT], rows[CUT:]] if mask == 3 else [rows]
            left[mask] = [swap(part, low) for part in parts]

    right = local(
        functools.partial(order_kernel, masks),
        shape((row_count * OWN, NORB), jnp.bfloat16),
        my_row.reshape(1).astype(jnp.int32),
        *passed_on,
        *mirrored,
    )
    def partial_sum(mask, *parts, **options):
        return block_sum(left[mask], right, tiles[mask], *parts, **options)

    short, wide = jnp.bfloat16, jnp.float32
    first_two, last_two = partial_sum(2, (CUT, wide), (OWN - CUT, short))
    last_two_there = swap(last_two, 2)
    first, last = left[3]
    first, _ = lax.optimization_barrier((first, last_two))
    (first_three,) = block_sum([first], right, tiles[3], (CUT, short))
    handed = swap(first_three, 1)
    last, _ = lax.optimization_barrier((last, first_three))
    (last_three,) = block_sum([last], right, tiles[3], (OWN - CUT, short), at=CUT)
    arrived, firsts = [swap(last_three, 3)], [CUT]
    first_both = local(add_kernel, shape(first_two.shape, short), first_two, handed)
    arrived.append(swap(first_both, 2))
    firsts.append(0)
    left[1][0], _ = lax.optimization_barrier((left[1][0], last_three))
    for mask in [1, *range(4, col_count)]:
        arrived.append(swap(partial_sum(mask, (OWN, short))[0], mask))
        firsts.append(0)
    (own_sum,) = partial_sum(0, (OWN, wide), earlier=[last_two_there], flops=10**10)
    picked = local(
        functools.partial(select_kernel, per_owner, firsts),
        shape((LIST, NORB), jnp.bfloat16),
        wanted,
        own_sum,
        *arrived,
    )
    chosen = lax.all_to_all(
        picked.reshape(box_total, per_owner, NORB),
        ("row", "col"),
        split_axis=0,
        concat_axis=0,
        tiled=True,
    ).reshape(LIST, NORB)
    box, count = interp.shape[0], 4
    return pl.pallas_call(
        apply_kernel,
        out_shape=jax.ShapeDtypeStruct((box, NORB), jnp.float32),
        in_specs=[vmem(), vmem()],
        out_specs=hbm(),
        scratch_shapes=[
            pltpu.VMEM((count, box // count, NORB), jnp.float32),
            pltpu.SemaphoreType.DMA((count,)),
        ],
        compiler_params=params(),
    )(interp, chosen)


def solution(mesh):
    return jax.shard_map(
        shards,
        mesh=mesh,
        in_specs=(
            P(("row", "col"), None),
            P("row", "col"),
            P(("row", "col"), None),
            P(),
            P(),
            P(("row", "col"), None),
            P(("row", "col"), None),
        ),
        out_specs=P(("row", "col"), None),
        check_vma=False,
    )
```

```python
import functools

import jax
import jax.numpy as jnp
from jax import lax
from jax.experimental import pallas as pl
from jax.experimental.pallas import tpu as pltpu
from jax.sharding import PartitionSpec as P

NORB = 512
LIST = 1024
OWN = 256
SLOTS = 768
LANES = 128
CUT = 96
VMEM_LIMIT = 48 * 1024 * 1024
PICK_LIMIT = 60 * 1024 * 1024


def vmem():
    return pl.BlockSpec(memory_space=pltpu.VMEM)


def smem():
    return pl.BlockSpec(memory_space=pltpu.SMEM)


def hbm():
    return pl.BlockSpec(memory_space=pltpu.HBM)


def params(limit=VMEM_LIMIT):
    return pltpu.CompilerParams(vmem_limit_bytes=limit)


def pick_kernel(
    box_total, capacity, counts_hbm, grid_hbm, owner_hbm, listed_hbm, orbitals_hbm, result,
    counts, grid_rows, owner_map, listed, orbitals, out, sems, out_sems,
):
    copies = [
        pltpu.make_async_copy(source, target, sems.at[n])
        for n, (source, target) in enumerate(
            [
                (counts_hbm, counts),
                (grid_hbm, grid_rows),
                (owner_hbm, owner_map),
                (listed_hbm, listed),
                (orbitals_hbm, orbitals),
            ]
        )
    ]
    for copy in copies:
        copy.start()
    targets = box_total * capacity
    my_box = lax.axis_index("row") * lax.axis_size("col") + lax.axis_index("col")
    copies[0].wait()
    start = jnp.int32(0)
    for b in range(box_total):
        start = start + jnp.where(b < my_box, counts[b], 0)
    stop = start + counts[my_box]
    first = start // LANES
    shift = start - first * LANES
    blocks = SLOTS // LANES + 1
    top = owner_map.shape[0] - 1
    lane = lax.broadcasted_iota(jnp.int32, (1, LANES), 1)
    copies[1].wait()
    copies[2].wait()
    turned = pltpu.roll(grid_rows[...], shift, 1)
    lane8 = lax.broadcasted_iota(jnp.int32, turned.shape, 1)
    lined = jnp.where(lane8 < shift, pltpu.roll(turned, 1, 0), turned)
    before = (
        lax.broadcasted_iota(jnp.int32, (LANES, LANES), 0)
        < lax.broadcasted_iota(jnp.int32, (LANES, LANES), 1)
    ).astype(jnp.bfloat16)
    owner_ids = lax.broadcasted_iota(jnp.int32, (box_total, LANES), 0)
    target_ids = lax.broadcasted_iota(jnp.int32, (targets, LANES), 0)
    base = jnp.zeros((box_total, 1), jnp.float32)
    found = jnp.zeros((targets, LANES), jnp.int32)
    for i in range(blocks):
        k = (first + i) * LANES + lane
        position = owner_map[pl.ds(jnp.minimum(first + i, top), 1), :]
        live = (k >= start) & (k < stop)
        owner = jnp.where(live, position // OWN, -1)
        member = (owner_ids == owner).astype(jnp.float32)
        inner = jnp.dot(member.astype(jnp.bfloat16), before, preferred_element_type=jnp.float32)
        rank = jnp.sum(member * (inner + base), axis=0, keepdims=True).astype(jnp.int32)
        base = base + jnp.sum(member, axis=1, keepdims=True)
        target = jnp.where(live, owner * capacity + rank, -1)
        found = found + jnp.where(target_ids == target, lined[i : i + 1, :] + 1, 0)
    source = jnp.sum(found.astype(jnp.float32), axis=1, keepdims=True).astype(jnp.int32) - 1
    copies[3].wait()
    per_owner = LIST // box_total
    fold = LANES // per_owner
    spread = jnp.broadcast_to(listed[...][:, None, :], (LIST // LANES, fold, LANES))
    spread = spread.reshape(box_total, LANES)
    phase = lax.broadcasted_iota(jnp.int32, spread.shape, 0) % fold
    indices = spread
    for q in range(1, fold):
        indices = jnp.where(phase == q, pltpu.roll(spread, LANES - q * per_owner, 1), indices)
    indices = indices.astype(jnp.float32).astype(jnp.bfloat16)
    tail = out.shape[1] - capacity * (NORB // LANES)
    out[:, capacity * (NORB // LANES) :, :] = jnp.broadcast_to(
        indices[:, None, :], (box_total, tail, LANES)
    )
    box = orbitals.shape[0]
    step = targets // 4
    sent = []
    copies[4].wait()
    for t in range(0, targets, step):
        hot = source[t : t + step] == lax.broadcasted_iota(jnp.int32, (step, box), 1)
        rows = jnp.dot(
            hot.astype(jnp.float32).astype(jnp.bfloat16),
            orbitals[...],
            preferred_element_type=jnp.float32,
        )
        owners = step // capacity
        packed = jnp.concatenate(
            [
                rows[:, c : c + LANES].reshape(owners, capacity, LANES)
                for c in range(0, NORB, LANES)
            ],
            axis=1,
        )
        first_owner = t // capacity
        out[first_owner : first_owner + owners, : packed.shape[1], :] = packed.astype(jnp.bfloat16)
        part = slice(first_owner, first_owner + owners)
        sent.append(
            pltpu.make_async_copy(out.at[part], result.at[part], out_sems.at[t // step])
        )
        sent[-1].start()
    for copy in sent:
        copy.wait()


def place_kernel(capacity, index, received, out, wanted):
    boxes = received.shape[0]
    packed = received[:, : capacity * (NORB // LANES), :].astype(jnp.float32)
    rows = jnp.concatenate(
        [
            packed[:, c * capacity : (c + 1) * capacity, :].reshape(boxes * capacity, LANES)
            for c in range(NORB // LANES)
        ],
        axis=1,
    ).astype(jnp.bfloat16)
    hot = index[...] == lax.broadcasted_iota(jnp.int32, (index.shape[0], rows.shape[0]), 1)
    out[...] = jnp.dot(
        hot.astype(jnp.float32).astype(jnp.bfloat16), rows, preferred_element_type=jnp.float32
    ).astype(jnp.bfloat16)
    tail = received[:, capacity * (NORB // LANES) :, :].astype(jnp.float32)
    wanted[...] = tail[:, 0, :].astype(jnp.int32)


def join_kernel(*refs):
    out, at = refs[-1], 0
    for ref in refs[:-1]:
        out[at : at + ref.shape[0], :] = ref[...]
        at += ref.shape[0]


def hold_kernel(*refs):
    count = len(refs) // 2
    for source, target in zip(refs[:count], refs[count:]):
        target[...] = source[...]


def pair_block(left, right):
    return lax.dot_general(
        left, right, (((1,), (1,)), ((), ())), preferred_element_type=jnp.float32
    ).astype(jnp.bfloat16)


def order_kernel(masks, scalars, *refs):
    pieces, out = refs[:-1], refs[-1]
    places = [mask ^ parity for parity in (0, 1) for mask in masks]
    for ref in pieces:
        for n in range(ref.shape[0] // OWN):
            place = jnp.bitwise_xor(scalars[0], places.pop(0)) * OWN
            out[pl.ds(pl.multiple_of(place, OWN), OWN), :] = ref[n * OWN : (n + 1) * OWN, :]


def fetch_kernel(scalars, coulomb, *refs):
    outs, sems = refs[:-1], refs[-1]
    copies = []
    for n, out in enumerate(outs):
        source = pl.ds(pl.multiple_of(scalars[n] * OWN, OWN), OWN)
        copies.append(pltpu.make_async_copy(coulomb.at[source, :], out, sems.at[n]))
        copies[-1].start()
    for copy in copies:
        copy.wait()


def block_kernel(count, spans, at, *refs):
    lefts, right, tile = refs[:count], refs[count], refs[count + 1]
    earlier, outs, weighted = refs[count + 2 : -1 - len(spans)], refs[-1 - len(spans) : -1], refs[-1]
    left = jnp.concatenate([ref[...] for ref in lefts]) if count > 1 else lefts[0][...]
    rows = slice(at, at + left.shape[0])
    step = 512
    for t in range(0, right.shape[0], step):
        pair = pair_block(left, right[t : t + step, :]).astype(jnp.float32)
        weighted[:, t : t + step] = (
            pair * tile[rows, t : t + step].astype(jnp.float32)
        ).astype(jnp.bfloat16)
    total = jnp.dot(weighted[...], right[...], preferred_element_type=jnp.float32)
    for out, (low, high) in zip(outs, spans):
        out[...] = total[low:high, :].astype(out.dtype)
    for ref in earlier:
        low = total.shape[0] - ref.shape[0]
        outs[0][low:, :] = total[low:, :] + ref[...].astype(jnp.float32)


def add_kernel(one, other, out):
    out[...] = (one[...] + other[...].astype(jnp.float32)).astype(out.dtype)


def block_sum(lefts, right, tile, *parts, at=0, earlier=(), flops=0):
    spans, low = [], 0
    for rows, _ in parts:
        spans.append((low, low + rows))
        low += rows
    return local(
        functools.partial(block_kernel, len(lefts), spans, at),
        tuple(jax.ShapeDtypeStruct((rows, NORB), dtype) for rows, dtype in parts),
        *lefts,
        right,
        tile,
        *earlier,
        flops=flops,
        scratch=[pltpu.VMEM((low, right.shape[0]), jnp.bfloat16)],
    )


def local(kernel, out, *args, flops=0, far=None, scratch=()):
    def spec(n, a):
        if n == far:
            return hbm()
        return smem() if a.ndim == 1 else vmem()

    return pl.pallas_call(
        kernel,
        out_shape=out,
        in_specs=[spec(n, a) for n, a in enumerate(args)],
        out_specs=jax.tree.map(lambda _: vmem(), out),
        scratch_shapes=scratch,
        compiler_params=params(),
        cost_estimate=pl.CostEstimate(flops=flops, bytes_accessed=0, transcendentals=0),
    )(*args)


def select_kernel(per_owner, firsts, index, own, *refs):
    boxes = index.shape[0]
    spread = jnp.broadcast_to(index[...][:, None, :], (boxes, per_owner, LANES))
    diagonal = lax.broadcasted_iota(jnp.int32, spread.shape, 1) == lax.broadcasted_iota(
        jnp.int32, spread.shape, 2
    )
    picks = jnp.sum(jnp.where(diagonal, spread, 0).astype(jnp.float32), axis=2, keepdims=True)
    picks = picks.reshape(boxes * per_owner, 1).astype(jnp.int32)
    out = refs[-1]
    totals = []
    for low, high in ((0, CUT), (CUT, OWN)):
        total = own[low:high, :]
        for ref, first in zip(refs[:-1], firsts):
            if first <= low < first + ref.shape[0]:
                total = total + ref[low - first : high - first, :].astype(jnp.float32)
        totals.append(total.astype(jnp.bfloat16))
    projected = jnp.concatenate(totals)
    hot = picks == lax.broadcasted_iota(jnp.int32, (boxes * per_owner, OWN), 1)
    out[...] = jnp.dot(
        hot.astype(jnp.float32).astype(jnp.bfloat16), projected, preferred_element_type=jnp.float32
    ).astype(jnp.bfloat16)


def apply_kernel(interp, chosen, out, parts, sems):
    rows = parts.shape[1]
    copies = []
    for n in range(parts.shape[0]):
        parts[n] = -jnp.dot(
            interp[n * rows : (n + 1) * rows, :], chosen[...], preferred_element_type=jnp.float32
        )
        target = out.at[n * rows : (n + 1) * rows, :]
        copies.append(pltpu.make_async_copy(parts.at[n], target, sems.at[n]))
        copies[-1].start()
    for copy in copies:
        copy.wait()


def shards(orbitals, coulomb, interp, box_counts, owner_map, grid_rows, listed):
    row_count = lax.axis_size("row")
    col_count = lax.axis_size("col")
    box_total = row_count * col_count
    point_total = OWN * box_total
    capacity = (SLOTS + box_total - 1) // box_total
    per_owner = LIST // box_total
    my_row, my_col = lax.axis_index("row"), lax.axis_index("col")
    my_box = my_row * col_count + my_col
    packed = capacity * (NORB // LANES)
    packed = (packed // 8 + 1) * 8
    outgoing = pl.pallas_call(
        functools.partial(pick_kernel, box_total, capacity),
        out_shape=jax.ShapeDtypeStruct((box_total, packed, LANES), jnp.bfloat16),
        in_specs=[hbm()] * 5,
        out_specs=hbm(),
        scratch_shapes=[
            pltpu.SMEM((box_total,), jnp.int32),
            pltpu.VMEM((grid_rows.shape[1] // LANES, LANES), jnp.int32),
            pltpu.VMEM((point_total // LANES, LANES), jnp.int32),
            pltpu.VMEM((LIST // LANES, LANES), jnp.int32),
            pltpu.VMEM(orbitals.shape, jnp.bfloat16),
            pltpu.VMEM((box_total, packed, LANES), jnp.bfloat16),
            pltpu.SemaphoreType.DMA((5,)),
            pltpu.SemaphoreType.DMA((4,)),
        ],
        compiler_params=params(PICK_LIMIT),
        cost_estimate=pl.CostEstimate(
            flops=2 * SLOTS * LIST * NORB, bytes_accessed=2 << 20, transcendentals=0
        ),
    )(
        box_counts,
        grid_rows.reshape(grid_rows.shape[1] // LANES, LANES),
        owner_map.reshape(point_total // LANES, LANES),
        listed.reshape(LIST // LANES, LANES),
        orbitals,
    )
    received = lax.all_to_all(
        outgoing, ("row", "col"), split_axis=0, concat_axis=0, tiled=True
    )

    wanted_pos = my_box * OWN + jnp.arange(OWN, dtype=jnp.int32)
    all_listing = jnp.arange(point_total, dtype=jnp.int32)
    my_points = jnp.sum(
        jnp.where(owner_map[None, :] == wanted_pos[:, None], all_listing[None, :], 0), axis=1
    )
    box_ends = jnp.cumsum(box_counts)
    source = jnp.sum((my_points[:, None] >= box_ends[None, :]).astype(jnp.int32), axis=1)
    earlier = (source[:, None] == source[None, :]) & (my_points[None, :] < my_points[:, None])
    source_rank = jnp.sum(earlier.astype(jnp.int32), axis=1)
    index = (source * capacity + source_rank).reshape(OWN, 1)
    owned_rows, wanted = pl.pallas_call(
        functools.partial(place_kernel, capacity),
        out_shape=(
            jax.ShapeDtypeStruct((OWN, NORB), jnp.bfloat16),
            jax.ShapeDtypeStruct((box_total, LANES), jnp.int32),
        ),
        in_specs=[vmem(), vmem()],
        out_specs=(vmem(), vmem()),
        compiler_params=params(),
    )(index, received)

    def swap(rows, mask):
        return lax.ppermute(rows, "col", [(i, i ^ mask) for i in range(col_count)])

    def join(*rows):
        total = sum(r.shape[0] for r in rows)
        return local(join_kernel, jax.ShapeDtypeStruct((total, NORB), rows[0].dtype), *rows)

    def flip(rows, mask):
        return lax.ppermute(rows, "row", [(i, i ^ mask) for i in range(row_count)])

    half = OWN // 2
    left = {0: [owned_rows]}
    for mask in range(1, col_count):
        if mask & (mask - 1) == 0:
            left[mask] = [swap(owned_rows, mask)]

    whole = {0: owned_rows}
    single = [1 << b for b in range(1, row_count.bit_length() - 1)]
    double = [mask for mask in range(2, row_count, 2) if mask not in single]
    for mask in single:
        whole[mask] = flip(owned_rows, mask)
    tiles = local(
        fetch_kernel,
        tuple(jax.ShapeDtypeStruct((OWN, row_count * OWN), jnp.bfloat16) for _ in range(col_count)),
        jnp.bitwise_xor(my_col, jnp.arange(col_count)).astype(jnp.int32),
        coulomb,
        far=1,
        scratch=[pltpu.SemaphoreType.DMA((col_count,))],
    )

    whole[single[0]], *tiles = lax.optimization_barrier((whole[single[0]], *tiles))
    passed_on = [owned_rows, join(*[whole[mask] for mask in single])]
    for mask in double:
        low, high = mask & -mask, 1 << (mask.bit_length() - 1)
        whole[mask] = join(
            flip(whole[mask ^ high][:half], high), flip(whole[mask ^ low][half:], low)
        )
    if double:
        passed_on.append(join(*[whole[mask] for mask in double]))
    masks = [0] + single + double
    shape = jax.ShapeDtypeStruct
    mirrored = [flip(rows, 1) for rows in passed_on]
    direct = [mask for mask in left if mask]
    held = local(
        hold_kernel,
        tuple(shape(owned_rows.shape, owned_rows.dtype) for _ in direct),
        *[left[mask][0] for mask in direct],
        flops=20 * 10**9,
    )
    *held, mirrored[0] = lax.optimization_barrier((*held, mirrored[0]))
    left.update((mask, [rows]) for mask, rows in zip(direct, held))
    for mask in range(3, col_count):
        if mask not in left:
            low = mask & -mask
            (rows,) = left[mask ^ low]
            parts = [rows[:CUT], rows[CUT:]] if mask == 3 else [rows]
            left[mask] = [swap(part, low) for part in parts]

    right = local(
        functools.partial(order_kernel, masks),
        shape((row_count * OWN, NORB), jnp.bfloat16),
        my_row.reshape(1).astype(jnp.int32),
        *passed_on,
        *mirrored,
    )
    def partial_sum(mask, *parts, **options):
        return block_sum(left[mask], right, tiles[mask], *parts, **options)

    short, wide = jnp.bfloat16, jnp.float32
    first_two, last_two = partial_sum(2, (CUT, wide), (OWN - CUT, short))
    last_two_there = swap(last_two, 2)
    first, last = left[3]
    first, _ = lax.optimization_barrier((first, last_two))
    (first_three,) = block_sum([first], right, tiles[3], (CUT, short))
    handed = swap(first_three, 1)
    last, _ = lax.optimization_barrier((last, first_three))
    (last_three,) = block_sum([last], right, tiles[3], (OWN - CUT, short), at=CUT)
    arrived, firsts = [swap(last_three, 3)], [CUT]
    first_both = local(add_kernel, shape(first_two.shape, short), first_two, handed)
    arrived.append(swap(first_both, 2))
    firsts.append(0)
    left[1][0], _ = lax.optimization_barrier((left[1][0], last_three))
    for mask in [1, *range(4, col_count)]:
        arrived.append(swap(partial_sum(mask, (OWN, short))[0], mask))
        firsts.append(0)
    (own_sum,) = partial_sum(0, (OWN, wide), earlier=[last_two_there], flops=10**10)
    picked = local(
        functools.partial(select_kernel, per_owner, firsts),
        shape((LIST, NORB), jnp.bfloat16),
        wanted,
        own_sum,
        *arrived,
    )
    chosen = lax.all_to_all(
        picked.reshape(box_total, per_owner, NORB),
        ("row", "col"),
        split_axis=0,
        concat_axis=0,
        tiled=True,
    ).reshape(LIST, NORB)
    box, count = interp.shape[0], 4
    return pl.pallas_call(
        apply_kernel,
        out_shape=jax.ShapeDtypeStruct((box, NORB), jnp.float32),
        in_specs=[vmem(), vmem()],
        out_specs=hbm(),
        scratch_shapes=[
            pltpu.VMEM((count, box // count, NORB), jnp.float32),
            pltpu.SemaphoreType.DMA((count,)),
        ],
        compiler_params=params(),
    )(interp, chosen)


def solution(mesh):
    return jax.shard_map(
        shards,
        mesh=mesh,
        in_specs=(
            P(("row", "col"), None),
            P("row", "col"),
            P(("row", "col"), None),
            P(),
            P(),
            P(("row", "col"), None),
            P(("row", "col"), None),
        ),
        out_specs=P(("row", "col"), None),
        check_vma=False,
    )
```

```python
import functools

import jax
import jax.numpy as jnp
from jax import lax
from jax.experimental import pallas as pl
from jax.experimental.pallas import tpu as pltpu
from jax.sharding import PartitionSpec as P

NORB = 512
LIST = 1024
OWN = 256
SLOTS = 768
LANES = 128
CUT = 96
VMEM_LIMIT = 48 * 1024 * 1024
PICK_LIMIT = 60 * 1024 * 1024


def vmem():
    return pl.BlockSpec(memory_space=pltpu.VMEM)


def smem():
    return pl.BlockSpec(memory_space=pltpu.SMEM)


def hbm():
    return pl.BlockSpec(memory_space=pltpu.HBM)


def params(limit=VMEM_LIMIT):
    return pltpu.CompilerParams(vmem_limit_bytes=limit)


def pick_kernel(
    box_total, capacity, counts_hbm, grid_hbm, owner_hbm, listed_hbm, orbitals_hbm, result,
    counts, grid_rows, owner_map, listed, orbitals, out, sems, out_sems,
):
    copies = [
        pltpu.make_async_copy(source, target, sems.at[n])
        for n, (source, target) in enumerate(
            [
                (counts_hbm, counts),
                (grid_hbm, grid_rows),
                (owner_hbm, owner_map),
                (listed_hbm, listed),
                (orbitals_hbm, orbitals),
            ]
        )
    ]
    for copy in copies:
        copy.start()
    targets = box_total * capacity
    my_box = lax.axis_index("row") * lax.axis_size("col") + lax.axis_index("col")
    copies[0].wait()
    start = jnp.int32(0)
    for b in range(box_total):
        start = start + jnp.where(b < my_box, counts[b], 0)
    stop = start + counts[my_box]
    first = start // LANES
    shift = start - first * LANES
    blocks = SLOTS // LANES + 1
    top = owner_map.shape[0] - 1
    lane = lax.broadcasted_iota(jnp.int32, (1, LANES), 1)
    copies[1].wait()
    copies[2].wait()
    turned = pltpu.roll(grid_rows[...], shift, 1)
    lane8 = lax.broadcasted_iota(jnp.int32, turned.shape, 1)
    lined = jnp.where(lane8 < shift, pltpu.roll(turned, 1, 0), turned)
    before = (
        lax.broadcasted_iota(jnp.int32, (LANES, LANES), 0)
        < lax.broadcasted_iota(jnp.int32, (LANES, LANES), 1)
    ).astype(jnp.bfloat16)
    owner_ids = lax.broadcasted_iota(jnp.int32, (box_total, LANES), 0)
    target_ids = lax.broadcasted_iota(jnp.int32, (targets, LANES), 0)
    base = jnp.zeros((box_total, 1), jnp.float32)
    found = jnp.zeros((targets, LANES), jnp.int32)
    for i in range(blocks):
        k = (first + i) * LANES + lane
        position = owner_map[pl.ds(jnp.minimum(first + i, top), 1), :]
        live = (k >= start) & (k < stop)
        owner = jnp.where(live, position // OWN, -1)
        member = (owner_ids == owner).astype(jnp.float32)
        inner = jnp.dot(member.astype(jnp.bfloat16), before, preferred_element_type=jnp.float32)
        rank = jnp.sum(member * (inner + base), axis=0, keepdims=True).astype(jnp.int32)
        base = base + jnp.sum(member, axis=1, keepdims=True)
        target = jnp.where(live, owner * capacity + rank, -1)
        found = found + jnp.where(target_ids == target, lined[i : i + 1, :] + 1, 0)
    source = jnp.sum(found.astype(jnp.float32), axis=1, keepdims=True).astype(jnp.int32) - 1
    copies[3].wait()
    per_owner = LIST // box_total
    fold = LANES // per_owner
    spread = jnp.broadcast_to(listed[...][:, None, :], (LIST // LANES, fold, LANES))
    spread = spread.reshape(box_total, LANES)
    phase = lax.broadcasted_iota(jnp.int32, spread.shape, 0) % fold
    indices = spread
    for q in range(1, fold):
        indices = jnp.where(phase == q, pltpu.roll(spread, LANES - q * per_owner, 1), indices)
    indices = indices.astype(jnp.float32).astype(jnp.bfloat16)
    tail = out.shape[1] - capacity * (NORB // LANES)
    out[:, capacity * (NORB // LANES) :, :] = jnp.broadcast_to(
        indices[:, None, :], (box_total, tail, LANES)
    )
    box = orbitals.shape[0]
    step = targets // 4
    sent = []
    copies[4].wait()
    for t in range(0, targets, step):
        hot = source[t : t + step] == lax.broadcasted_iota(jnp.int32, (step, box), 1)
        rows = jnp.dot(
            hot.astype(jnp.float32).astype(jnp.bfloat16),
            orbitals[...],
            preferred_element_type=jnp.float32,
        )
        owners = step // capacity
        packed = jnp.concatenate(
            [
                rows[:, c : c + LANES].reshape(owners, capacity, LANES)
                for c in range(0, NORB, LANES)
            ],
            axis=1,
        )
        first_owner = t // capacity
        out[first_owner : first_owner + owners, : packed.shape[1], :] = packed.astype(jnp.bfloat16)
        part = slice(first_owner, first_owner + owners)
        sent.append(
            pltpu.make_async_copy(out.at[part], result.at[part], out_sems.at[t // step])
        )
        sent[-1].start()
    for copy in sent:
        copy.wait()


def place_kernel(capacity, index, received, out, wanted):
    boxes = received.shape[0]
    packed = received[:, : capacity * (NORB // LANES), :].astype(jnp.float32)
    rows = jnp.concatenate(
        [
            packed[:, c * capacity : (c + 1) * capacity, :].reshape(boxes * capacity, LANES)
            for c in range(NORB // LANES)
        ],
        axis=1,
    ).astype(jnp.bfloat16)
    hot = index[...] == lax.broadcasted_iota(jnp.int32, (index.shape[0], rows.shape[0]), 1)
    out[...] = jnp.dot(
        hot.astype(jnp.float32).astype(jnp.bfloat16), rows, preferred_element_type=jnp.float32
    ).astype(jnp.bfloat16)
    tail = received[:, capacity * (NORB // LANES) :, :].astype(jnp.float32)
    wanted[...] = tail[:, 0, :].astype(jnp.int32)


def join_kernel(*refs):
    out, at = refs[-1], 0
    for ref in refs[:-1]:
        out[at : at + ref.shape[0], :] = ref[...]
        at += ref.shape[0]


def hold_kernel(*refs):
    count = len(refs) // 2
    for source, target in zip(refs[:count], refs[count:]):
        target[...] = source[...]


def pair_block(left, right):
    return lax.dot_general(
        left, right, (((1,), (1,)), ((), ())), preferred_element_type=jnp.float32
    ).astype(jnp.bfloat16)


def turn(mask):
    return mask & ~6 | (mask & 2) << 1 | (mask & 4) >> 1


def order_kernel(masks, scalars, *refs):
    pieces, out = refs[:-1], refs[-1]
    me = scalars[0]
    odd = lax.rem(me, 2) == 1
    places = [jnp.where(odd, turn(mask), mask) for mask in masks]
    places += [jnp.where(odd, mask, turn(mask)) ^ 1 for mask in masks]
    for ref in pieces:
        for n in range(ref.shape[0] // OWN):
            place = jnp.bitwise_xor(me, places.pop(0)) * OWN
            out[pl.ds(pl.multiple_of(place, OWN), OWN), :] = ref[n * OWN : (n + 1) * OWN, :]


def fetch_kernel(scalars, coulomb, *refs):
    outs, sems = refs[:-1], refs[-1]
    copies = []
    for n, out in enumerate(outs):
        source = pl.ds(pl.multiple_of(scalars[n] * OWN, OWN), OWN)
        copies.append(pltpu.make_async_copy(coulomb.at[source, :], out, sems.at[n]))
        copies[-1].start()
    for copy in copies:
        copy.wait()


def block_kernel(count, spans, at, *refs):
    lefts, right, tile = refs[:count], refs[count], refs[count + 1]
    earlier, outs, weighted = refs[count + 2 : -1 - len(spans)], refs[-1 - len(spans) : -1], refs[-1]
    left = jnp.concatenate([ref[...] for ref in lefts]) if count > 1 else lefts[0][...]
    rows = slice(at, at + left.shape[0])
    step = 512
    for t in range(0, right.shape[0], step):
        pair = pair_block(left, right[t : t + step, :]).astype(jnp.float32)
        weighted[:, t : t + step] = (
            pair * tile[rows, t : t + step].astype(jnp.float32)
        ).astype(jnp.bfloat16)
    total = jnp.dot(weighted[...], right[...], preferred_element_type=jnp.float32)
    for out, (low, high) in zip(outs, spans):
        out[...] = total[low:high, :].astype(out.dtype)
    for ref in earlier:
        low = total.shape[0] - ref.shape[0]
        outs[0][low:, :] = total[low:, :] + ref[...].astype(jnp.float32)


def add_kernel(one, other, out):
    out[...] = (one[...] + other[...].astype(jnp.float32)).astype(out.dtype)


def block_sum(lefts, right, tile, *parts, at=0, earlier=(), flops=0):
    spans, low = [], 0
    for rows, _ in parts:
        spans.append((low, low + rows))
        low += rows
    return local(
        functools.partial(block_kernel, len(lefts), spans, at),
        tuple(jax.ShapeDtypeStruct((rows, NORB), dtype) for rows, dtype in parts),
        *lefts,
        right,
        tile,
        *earlier,
        flops=flops,
        scratch=[pltpu.VMEM((low, right.shape[0]), jnp.bfloat16)],
    )


def local(kernel, out, *args, flops=0, far=None, scratch=()):
    def spec(n, a):
        if n == far:
            return hbm()
        return smem() if a.ndim == 1 else vmem()

    return pl.pallas_call(
        kernel,
        out_shape=out,
        in_specs=[spec(n, a) for n, a in enumerate(args)],
        out_specs=jax.tree.map(lambda _: vmem(), out),
        scratch_shapes=scratch,
        compiler_params=params(),
        cost_estimate=pl.CostEstimate(flops=flops, bytes_accessed=0, transcendentals=0),
    )(*args)


def select_kernel(per_owner, firsts, index, own, *refs):
    boxes = index.shape[0]
    spread = jnp.broadcast_to(index[...][:, None, :], (boxes, per_owner, LANES))
    diagonal = lax.broadcasted_iota(jnp.int32, spread.shape, 1) == lax.broadcasted_iota(
        jnp.int32, spread.shape, 2
    )
    picks = jnp.sum(jnp.where(diagonal, spread, 0).astype(jnp.float32), axis=2, keepdims=True)
    picks = picks.reshape(boxes * per_owner, 1).astype(jnp.int32)
    out = refs[-1]
    totals = []
    for low, high in ((0, CUT), (CUT, OWN)):
        total = own[low:high, :]
        for ref, first in zip(refs[:-1], firsts):
            if first <= low < first + ref.shape[0]:
                total = total + ref[low - first : high - first, :].astype(jnp.float32)
        totals.append(total.astype(jnp.bfloat16))
    projected = jnp.concatenate(totals)
    hot = picks == lax.broadcasted_iota(jnp.int32, (boxes * per_owner, OWN), 1)
    out[...] = jnp.dot(
        hot.astype(jnp.float32).astype(jnp.bfloat16), projected, preferred_element_type=jnp.float32
    ).astype(jnp.bfloat16)


def apply_kernel(interp, chosen, out, parts, sems):
    rows = parts.shape[1]
    copies = []
    for n in range(parts.shape[0]):
        parts[n] = -jnp.dot(
            interp[n * rows : (n + 1) * rows, :], chosen[...], preferred_element_type=jnp.float32
        )
        target = out.at[n * rows : (n + 1) * rows, :]
        copies.append(pltpu.make_async_copy(parts.at[n], target, sems.at[n]))
        copies[-1].start()
    for copy in copies:
        copy.wait()


def shards(orbitals, coulomb, interp, box_counts, owner_map, grid_rows, listed):
    row_count = lax.axis_size("row")
    col_count = lax.axis_size("col")
    box_total = row_count * col_count
    point_total = OWN * box_total
    capacity = (SLOTS + box_total - 1) // box_total
    per_owner = LIST // box_total
    my_row, my_col = lax.axis_index("row"), lax.axis_index("col")
    my_box = my_row * col_count + my_col
    packed = capacity * (NORB // LANES)
    packed = (packed // 8 + 1) * 8
    outgoing = pl.pallas_call(
        functools.partial(pick_kernel, box_total, capacity),
        out_shape=jax.ShapeDtypeStruct((box_total, packed, LANES), jnp.bfloat16),
        in_specs=[hbm()] * 5,
        out_specs=hbm(),
        scratch_shapes=[
            pltpu.SMEM((box_total,), jnp.int32),
            pltpu.VMEM((grid_rows.shape[1] // LANES, LANES), jnp.int32),
            pltpu.VMEM((point_total // LANES, LANES), jnp.int32),
            pltpu.VMEM((LIST // LANES, LANES), jnp.int32),
            pltpu.VMEM(orbitals.shape, jnp.bfloat16),
            pltpu.VMEM((box_total, packed, LANES), jnp.bfloat16),
            pltpu.SemaphoreType.DMA((5,)),
            pltpu.SemaphoreType.DMA((4,)),
        ],
        compiler_params=params(PICK_LIMIT),
        cost_estimate=pl.CostEstimate(
            flops=2 * SLOTS * LIST * NORB, bytes_accessed=2 << 20, transcendentals=0
        ),
    )(
        box_counts,
        grid_rows.reshape(grid_rows.shape[1] // LANES, LANES),
        owner_map.reshape(point_total // LANES, LANES),
        listed.reshape(LIST // LANES, LANES),
        orbitals,
    )
    received = lax.all_to_all(
        outgoing, ("row", "col"), split_axis=0, concat_axis=0, tiled=True
    )

    wanted_pos = my_box * OWN + jnp.arange(OWN, dtype=jnp.int32)
    all_listing = jnp.arange(point_total, dtype=jnp.int32)
    my_points = jnp.sum(
        jnp.where(owner_map[None, :] == wanted_pos[:, None], all_listing[None, :], 0), axis=1
    )
    box_ends = jnp.cumsum(box_counts)
    source = jnp.sum((my_points[:, None] >= box_ends[None, :]).astype(jnp.int32), axis=1)
    earlier = (source[:, None] == source[None, :]) & (my_points[None, :] < my_points[:, None])
    source_rank = jnp.sum(earlier.astype(jnp.int32), axis=1)
    index = (source * capacity + source_rank).reshape(OWN, 1)
    owned_rows, wanted = pl.pallas_call(
        functools.partial(place_kernel, capacity),
        out_shape=(
            jax.ShapeDtypeStruct((OWN, NORB), jnp.bfloat16),
            jax.ShapeDtypeStruct((box_total, LANES), jnp.int32),
        ),
        in_specs=[vmem(), vmem()],
        out_specs=(vmem(), vmem()),
        compiler_params=params(),
    )(index, received)

    def swap(rows, mask):
        return lax.ppermute(rows, "col", [(i, i ^ mask) for i in range(col_count)])

    def join(*rows):
        total = sum(r.shape[0] for r in rows)
        return local(join_kernel, jax.ShapeDtypeStruct((total, NORB), rows[0].dtype), *rows)

    def flip(rows, mask):
        return lax.ppermute(
            rows, "row", [(i, i ^ (turn(mask) if i & 1 else mask)) for i in range(row_count)]
        )

    half = OWN // 2
    left = {0: [owned_rows]}
    for mask in range(1, col_count):
        if mask & (mask - 1) == 0:
            left[mask] = [swap(owned_rows, mask)]

    whole = {0: owned_rows}
    single = [1 << b for b in range(1, row_count.bit_length() - 1)]
    double = [mask for mask in range(2, row_count, 2) if mask not in single]
    for mask in single:
        whole[mask] = flip(owned_rows, mask)
    tiles = local(
        fetch_kernel,
        tuple(jax.ShapeDtypeStruct((OWN, row_count * OWN), jnp.bfloat16) for _ in range(col_count)),
        jnp.bitwise_xor(my_col, jnp.arange(col_count)).astype(jnp.int32),
        coulomb,
        far=1,
        scratch=[pltpu.SemaphoreType.DMA((col_count,))],
    )

    whole[single[0]], *tiles = lax.optimization_barrier((whole[single[0]], *tiles))
    passed_on = [owned_rows, join(*[whole[mask] for mask in single])]
    for mask in double:
        low, high = mask & -mask, 1 << (mask.bit_length() - 1)
        whole[mask] = join(
            flip(whole[mask ^ high][:half], high), flip(whole[mask ^ low][half:], low)
        )
    if double:
        passed_on.append(join(*[whole[mask] for mask in double]))
    masks = [0] + single + double
    shape = jax.ShapeDtypeStruct
    mirrored = [flip(rows, 1) for rows in passed_on]
    direct = [mask for mask in left if mask]
    held = local(
        hold_kernel,
        tuple(shape(owned_rows.shape, owned_rows.dtype) for _ in direct),
        *[left[mask][0] for mask in direct],
        flops=20 * 10**9,
    )
    *held, mirrored[0] = lax.optimization_barrier((*held, mirrored[0]))
    left.update((mask, [rows]) for mask, rows in zip(direct, held))
    for mask in range(3, col_count):
        if mask not in left:
            low = mask & -mask
            (rows,) = left[mask ^ low]
            parts = [rows[:CUT], rows[CUT:]] if mask == 3 else [rows]
            left[mask] = [swap(part, low) for part in parts]

    right = local(
        functools.partial(order_kernel, masks),
        shape((row_count * OWN, NORB), jnp.bfloat16),
        my_row.reshape(1).astype(jnp.int32),
        *passed_on,
        *mirrored,
    )
    def partial_sum(mask, *parts, **options):
        return block_sum(left[mask], right, tiles[mask], *parts, **options)

    short, wide = jnp.bfloat16, jnp.float32
    first_two, last_two = partial_sum(2, (CUT, wide), (OWN - CUT, short))
    last_two_there = swap(last_two, 2)
    first, last = left[3]
    first, _ = lax.optimization_barrier((first, last_two))
    (first_three,) = block_sum([first], right, tiles[3], (CUT, short))
    handed = swap(first_three, 1)
    last, _ = lax.optimization_barrier((last, first_three))
    (last_three,) = block_sum([last], right, tiles[3], (OWN - CUT, short), at=CUT)
    arrived, firsts = [swap(last_three, 3)], [CUT]
    first_both = local(add_kernel, shape(first_two.shape, short), first_two, handed)
    arrived.append(swap(first_both, 2))
    firsts.append(0)
    left[1][0], _ = lax.optimization_barrier((left[1][0], last_three))
    for mask in [1, *range(4, col_count)]:
        arrived.append(swap(partial_sum(mask, (OWN, short))[0], mask))
        firsts.append(0)
    (own_sum,) = partial_sum(0, (OWN, wide), earlier=[last_two_there], flops=10**10)
    picked = local(
        functools.partial(select_kernel, per_owner, firsts),
        shape((LIST, NORB), jnp.bfloat16),
        wanted,
        own_sum,
        *arrived,
    )
    chosen = lax.all_to_all(
        picked.reshape(box_total, per_owner, NORB),
        ("row", "col"),
        split_axis=0,
        concat_axis=0,
        tiled=True,
    ).reshape(LIST, NORB)
    box, count = interp.shape[0], 4
    return pl.pallas_call(
        apply_kernel,
        out_shape=jax.ShapeDtypeStruct((box, NORB), jnp.float32),
        in_specs=[vmem(), vmem()],
        out_specs=hbm(),
        scratch_shapes=[
            pltpu.VMEM((count, box // count, NORB), jnp.float32),
            pltpu.SemaphoreType.DMA((count,)),
        ],
        compiler_params=params(),
    )(interp, chosen)


def solution(mesh):
    return jax.shard_map(
        shards,
        mesh=mesh,
        in_specs=(
            P(("row", "col"), None),
            P("row", "col"),
            P(("row", "col"), None),
            P(),
            P(),
            P(("row", "col"), None),
            P(("row", "col"), None),
        ),
        out_specs=P(("row", "col"), None),
        check_vma=False,
    )
```

```python
import functools

import jax
import jax.numpy as jnp
from jax import lax
from jax.experimental import pallas as pl
from jax.experimental.pallas import tpu as pltpu
from jax.sharding import PartitionSpec as P

NORB = 512
LIST = 1024
OWN = 256
SLOTS = 768
LANES = 128
CUT = 96
VMEM_LIMIT = 48 * 1024 * 1024
PICK_LIMIT = 60 * 1024 * 1024


def vmem():
    return pl.BlockSpec(memory_space=pltpu.VMEM)


def smem():
    return pl.BlockSpec(memory_space=pltpu.SMEM)


def hbm():
    return pl.BlockSpec(memory_space=pltpu.HBM)


def params(limit=VMEM_LIMIT):
    return pltpu.CompilerParams(vmem_limit_bytes=limit)


def pick_kernel(
    box_total, capacity, counts_hbm, grid_hbm, owner_hbm, listed_hbm, orbitals_hbm, result,
    counts, grid_rows, owner_map, listed, orbitals, out, sems, out_sems,
):
    copies = [
        pltpu.make_async_copy(source, target, sems.at[n])
        for n, (source, target) in enumerate(
            [
                (counts_hbm, counts),
                (grid_hbm, grid_rows),
                (owner_hbm, owner_map),
                (listed_hbm, listed),
                (orbitals_hbm, orbitals),
            ]
        )
    ]
    for copy in copies:
        copy.start()
    targets = box_total * capacity
    my_box = lax.axis_index("row") * lax.axis_size("col") + lax.axis_index("col")
    copies[0].wait()
    start = jnp.int32(0)
    for b in range(box_total):
        start = start + jnp.where(b < my_box, counts[b], 0)
    stop = start + counts[my_box]
    first = start // LANES
    shift = start - first * LANES
    blocks = SLOTS // LANES + 1
    top = owner_map.shape[0] - 1
    lane = lax.broadcasted_iota(jnp.int32, (1, LANES), 1)
    copies[1].wait()
    copies[2].wait()
    turned = pltpu.roll(grid_rows[...], shift, 1)
    lane8 = lax.broadcasted_iota(jnp.int32, turned.shape, 1)
    lined = jnp.where(lane8 < shift, pltpu.roll(turned, 1, 0), turned)
    before = (
        lax.broadcasted_iota(jnp.int32, (LANES, LANES), 0)
        < lax.broadcasted_iota(jnp.int32, (LANES, LANES), 1)
    ).astype(jnp.bfloat16)
    owner_ids = lax.broadcasted_iota(jnp.int32, (box_total, LANES), 0)
    target_ids = lax.broadcasted_iota(jnp.int32, (targets, LANES), 0)
    base = jnp.zeros((box_total, 1), jnp.float32)
    found = jnp.zeros((targets, LANES), jnp.int32)
    for i in range(blocks):
        k = (first + i) * LANES + lane
        position = owner_map[pl.ds(jnp.minimum(first + i, top), 1), :]
        live = (k >= start) & (k < stop)
        owner = jnp.where(live, position // OWN, -1)
        member = (owner_ids == owner).astype(jnp.float32)
        inner = jnp.dot(member.astype(jnp.bfloat16), before, preferred_element_type=jnp.float32)
        rank = jnp.sum(member * (inner + base), axis=0, keepdims=True).astype(jnp.int32)
        base = base + jnp.sum(member, axis=1, keepdims=True)
        target = jnp.where(live, owner * capacity + rank, -1)
        found = found + jnp.where(target_ids == target, lined[i : i + 1, :] + 1, 0)
    source = jnp.sum(found.astype(jnp.float32), axis=1, keepdims=True).astype(jnp.int32) - 1
    copies[3].wait()
    per_owner = LIST // box_total
    fold = LANES // per_owner
    spread = jnp.broadcast_to(listed[...][:, None, :], (LIST // LANES, fold, LANES))
    spread = spread.reshape(box_total, LANES)
    phase = lax.broadcasted_iota(jnp.int32, spread.shape, 0) % fold
    indices = spread
    for q in range(1, fold):
        indices = jnp.where(phase == q, pltpu.roll(spread, LANES - q * per_owner, 1), indices)
    indices = indices.astype(jnp.float32).astype(jnp.bfloat16)
    tail = out.shape[1] - capacity * (NORB // LANES)
    out[:, capacity * (NORB // LANES) :, :] = jnp.broadcast_to(
        indices[:, None, :], (box_total, tail, LANES)
    )
    box = orbitals.shape[0]
    step = targets // 4
    sent = []
    copies[4].wait()
    for t in range(0, targets, step):
        hot = source[t : t + step] == lax.broadcasted_iota(jnp.int32, (step, box), 1)
        rows = jnp.dot(
            hot.astype(jnp.float32).astype(jnp.bfloat16),
            orbitals[...],
            preferred_element_type=jnp.float32,
        )
        owners = step // capacity
        packed = jnp.concatenate(
            [
                rows[:, c : c + LANES].reshape(owners, capacity, LANES)
                for c in range(0, NORB, LANES)
            ],
            axis=1,
        )
        first_owner = t // capacity
        out[first_owner : first_owner + owners, : packed.shape[1], :] = packed.astype(jnp.bfloat16)
        part = slice(first_owner, first_owner + owners)
        sent.append(
            pltpu.make_async_copy(out.at[part], result.at[part], out_sems.at[t // step])
        )
        sent[-1].start()
    for copy in sent:
        copy.wait()


def place_kernel(capacity, index, received, out, wanted):
    boxes = received.shape[0]
    packed = received[:, : capacity * (NORB // LANES), :].astype(jnp.float32)
    rows = jnp.concatenate(
        [
            packed[:, c * capacity : (c + 1) * capacity, :].reshape(boxes * capacity, LANES)
            for c in range(NORB // LANES)
        ],
        axis=1,
    ).astype(jnp.bfloat16)
    hot = index[...] == lax.broadcasted_iota(jnp.int32, (index.shape[0], rows.shape[0]), 1)
    out[...] = jnp.dot(
        hot.astype(jnp.float32).astype(jnp.bfloat16), rows, preferred_element_type=jnp.float32
    ).astype(jnp.bfloat16)
    tail = received[:, capacity * (NORB // LANES) :, :].astype(jnp.float32)
    wanted[...] = tail[:, 0, :].astype(jnp.int32)


def join_kernel(*refs):
    out, at = refs[-1], 0
    for ref in refs[:-1]:
        out[at : at + ref.shape[0], :] = ref[...]
        at += ref.shape[0]


def hold_kernel(*refs):
    count = len(refs) // 2
    for source, target in zip(refs[:count], refs[count:]):
        target[...] = source[...]


def pair_block(left, right):
    return lax.dot_general(
        left, right, (((1,), (1,)), ((), ())), preferred_element_type=jnp.float32
    ).astype(jnp.bfloat16)


def order_kernel(masks, scalars, *refs):
    pieces, out = refs[:-1], refs[-1]
    places = [mask ^ parity for parity in (0, 1) for mask in masks]
    for ref in pieces:
        for n in range(ref.shape[0] // OWN):
            place = jnp.bitwise_xor(scalars[0], places.pop(0)) * OWN
            out[pl.ds(pl.multiple_of(place, OWN), OWN), :] = ref[n * OWN : (n + 1) * OWN, :]


def fetch_kernel(scalars, coulomb, *refs):
    outs, sems = refs[:-1], refs[-1]
    copies = []
    for n, out in enumerate(outs):
        source = pl.ds(pl.multiple_of(scalars[n] * OWN, OWN), OWN)
        copies.append(pltpu.make_async_copy(coulomb.at[source, :], out, sems.at[n]))
        copies[-1].start()
    for copy in copies:
        copy.wait()


def block_kernel(count, spans, at, *refs):
    lefts, right, tile = refs[:count], refs[count], refs[count + 1]
    earlier, outs, weighted = refs[count + 2 : -1 - len(spans)], refs[-1 - len(spans) : -1], refs[-1]
    left = jnp.concatenate([ref[...] for ref in lefts]) if count > 1 else lefts[0][...]
    rows = slice(at, at + left.shape[0])
    step = 512
    for t in range(0, right.shape[0], step):
        pair = pair_block(left, right[t : t + step, :]).astype(jnp.float32)
        weighted[:, t : t + step] = (
            pair * tile[rows, t : t + step].astype(jnp.float32)
        ).astype(jnp.bfloat16)
    total = jnp.dot(weighted[...], right[...], preferred_element_type=jnp.float32)
    for out, (low, high) in zip(outs, spans):
        out[...] = total[low:high, :].astype(out.dtype)
    for ref in earlier:
        low = total.shape[0] - ref.shape[0]
        outs[0][low:, :] = total[low:, :] + ref[...].astype(jnp.float32)


def add_kernel(one, other, out):
    out[...] = (one[...] + other[...].astype(jnp.float32)).astype(out.dtype)


def block_sum(lefts, right, tile, *parts, at=0, earlier=(), flops=0):
    spans, low = [], 0
    for rows, _ in parts:
        spans.append((low, low + rows))
        low += rows
    return local(
        functools.partial(block_kernel, len(lefts), spans, at),
        tuple(jax.ShapeDtypeStruct((rows, NORB), dtype) for rows, dtype in parts),
        *lefts,
        right,
        tile,
        *earlier,
        flops=flops,
        scratch=[pltpu.VMEM((low, right.shape[0]), jnp.bfloat16)],
    )


def local(kernel, out, *args, flops=0, far=None, scratch=()):
    def spec(n, a):
        if n == far:
            return hbm()
        return smem() if a.ndim == 1 else vmem()

    return pl.pallas_call(
        kernel,
        out_shape=out,
        in_specs=[spec(n, a) for n, a in enumerate(args)],
        out_specs=jax.tree.map(lambda _: vmem(), out),
        scratch_shapes=scratch,
        compiler_params=params(),
        cost_estimate=pl.CostEstimate(flops=flops, bytes_accessed=0, transcendentals=0),
    )(*args)


def select_kernel(per_owner, firsts, index, own, *refs):
    boxes = index.shape[0]
    spread = jnp.broadcast_to(index[...][:, None, :], (boxes, per_owner, LANES))
    diagonal = lax.broadcasted_iota(jnp.int32, spread.shape, 1) == lax.broadcasted_iota(
        jnp.int32, spread.shape, 2
    )
    picks = jnp.sum(jnp.where(diagonal, spread, 0).astype(jnp.float32), axis=2, keepdims=True)
    picks = picks.reshape(boxes * per_owner, 1).astype(jnp.int32)
    out = refs[-1]
    totals = []
    for low, high in ((0, CUT), (CUT, OWN)):
        total = own[low:high, :]
        for ref, first in zip(refs[:-1], firsts):
            if first <= low < first + ref.shape[0]:
                total = total + ref[low - first : high - first, :].astype(jnp.float32)
        totals.append(total.astype(jnp.bfloat16))
    projected = jnp.concatenate(totals)
    hot = picks == lax.broadcasted_iota(jnp.int32, (boxes * per_owner, OWN), 1)
    out[...] = jnp.dot(
        hot.astype(jnp.float32).astype(jnp.bfloat16), projected, preferred_element_type=jnp.float32
    ).astype(jnp.bfloat16)


def apply_kernel(interp, chosen, out, parts, sems):
    rows = parts.shape[1]
    copies = []
    for n in range(parts.shape[0]):
        parts[n] = -jnp.dot(
            interp[n * rows : (n + 1) * rows, :], chosen[...], preferred_element_type=jnp.float32
        )
        target = out.at[n * rows : (n + 1) * rows, :]
        copies.append(pltpu.make_async_copy(parts.at[n], target, sems.at[n]))
        copies[-1].start()
    for copy in copies:
        copy.wait()


def shards(orbitals, coulomb, interp, box_counts, owner_map, grid_rows, listed):
    row_count = lax.axis_size("row")
    col_count = lax.axis_size("col")
    box_total = row_count * col_count
    point_total = OWN * box_total
    capacity = (SLOTS + box_total - 1) // box_total
    per_owner = LIST // box_total
    my_row, my_col = lax.axis_index("row"), lax.axis_index("col")
    my_box = my_row * col_count + my_col
    packed = capacity * (NORB // LANES)
    packed = (packed // 8 + 1) * 8
    outgoing = pl.pallas_call(
        functools.partial(pick_kernel, box_total, capacity),
        out_shape=jax.ShapeDtypeStruct((box_total, packed, LANES), jnp.bfloat16),
        in_specs=[hbm()] * 5,
        out_specs=hbm(),
        scratch_shapes=[
            pltpu.SMEM((box_total,), jnp.int32),
            pltpu.VMEM((grid_rows.shape[1] // LANES, LANES), jnp.int32),
            pltpu.VMEM((point_total // LANES, LANES), jnp.int32),
            pltpu.VMEM((LIST // LANES, LANES), jnp.int32),
            pltpu.VMEM(orbitals.shape, jnp.bfloat16),
            pltpu.VMEM((box_total, packed, LANES), jnp.bfloat16),
            pltpu.SemaphoreType.DMA((5,)),
            pltpu.SemaphoreType.DMA((4,)),
        ],
        compiler_params=params(PICK_LIMIT),
        cost_estimate=pl.CostEstimate(
            flops=2 * SLOTS * LIST * NORB, bytes_accessed=2 << 20, transcendentals=0
        ),
    )(
        box_counts,
        grid_rows.reshape(grid_rows.shape[1] // LANES, LANES),
        owner_map.reshape(point_total // LANES, LANES),
        listed.reshape(LIST // LANES, LANES),
        orbitals,
    )
    received = lax.all_to_all(
        outgoing, ("row", "col"), split_axis=0, concat_axis=0, tiled=True
    )

    wanted_pos = my_box * OWN + jnp.arange(OWN, dtype=jnp.int32)
    all_listing = jnp.arange(point_total, dtype=jnp.int32)
    my_points = jnp.sum(
        jnp.where(owner_map[None, :] == wanted_pos[:, None], all_listing[None, :], 0), axis=1
    )
    box_ends = jnp.cumsum(box_counts)
    source = jnp.sum((my_points[:, None] >= box_ends[None, :]).astype(jnp.int32), axis=1)
    earlier = (source[:, None] == source[None, :]) & (my_points[None, :] < my_points[:, None])
    source_rank = jnp.sum(earlier.astype(jnp.int32), axis=1)
    index = (source * capacity + source_rank).reshape(OWN, 1)
    owned_rows, wanted = pl.pallas_call(
        functools.partial(place_kernel, capacity),
        out_shape=(
            jax.ShapeDtypeStruct((OWN, NORB), jnp.bfloat16),
            jax.ShapeDtypeStruct((box_total, LANES), jnp.int32),
        ),
        in_specs=[vmem(), vmem()],
        out_specs=(vmem(), vmem()),
        compiler_params=params(),
    )(index, received)

    def swap(rows, mask):
        return lax.ppermute(rows, "col", [(i, i ^ mask) for i in range(col_count)])

    def join(*rows):
        total = sum(r.shape[0] for r in rows)
        return local(join_kernel, jax.ShapeDtypeStruct((total, NORB), rows[0].dtype), *rows)

    def flip(rows, mask):
        return lax.ppermute(rows, "row", [(i, i ^ mask) for i in range(row_count)])

    half = OWN // 2
    left = {0: [owned_rows]}
    for mask in range(1, col_count):
        if mask & (mask - 1) == 0:
            left[mask] = [swap(owned_rows, mask)]

    whole = {0: owned_rows}
    single = [1 << b for b in range(1, row_count.bit_length() - 1)]
    double = [mask for mask in range(2, row_count, 2) if mask not in single]
    for mask in single:
        whole[mask] = flip(owned_rows, mask)
    tiles = local(
        fetch_kernel,
        tuple(jax.ShapeDtypeStruct((OWN, row_count * OWN), jnp.bfloat16) for _ in range(col_count)),
        jnp.bitwise_xor(my_col, jnp.arange(col_count)).astype(jnp.int32),
        coulomb,
        far=1,
        scratch=[pltpu.SemaphoreType.DMA((col_count,))],
    )

    whole[single[0]], *tiles = lax.optimization_barrier((whole[single[0]], *tiles))
    passed_on = [owned_rows, join(*[whole[mask] for mask in single])]
    for mask in double:
        low, high = mask & -mask, 1 << (mask.bit_length() - 1)
        whole[mask] = join(
            flip(whole[mask ^ high][:half], high), flip(whole[mask ^ low][half:], low)
        )
    if double:
        passed_on.append(join(*[whole[mask] for mask in double]))
    masks = [0] + single + double
    shape = jax.ShapeDtypeStruct
    mirrored = [flip(rows, 1) for rows in passed_on]
    direct = [mask for mask in left if mask]
    held = local(
        hold_kernel,
        tuple(shape(owned_rows.shape, owned_rows.dtype) for _ in direct),
        *[left[mask][0] for mask in direct],
        flops=20 * 10**9,
    )
    left.update((mask, [rows]) for mask, rows in zip(direct, held))
    for mask in range(3, col_count):
        if mask not in left:
            low = mask & -mask
            (rows,) = left[mask ^ low]
            parts = [rows[:CUT], rows[CUT:]] if mask == 3 else [rows]
            left[mask] = [swap(part, low) for part in parts]

    right = local(
        functools.partial(order_kernel, masks),
        shape((row_count * OWN, NORB), jnp.bfloat16),
        my_row.reshape(1).astype(jnp.int32),
        *passed_on,
        *mirrored,
    )
    def partial_sum(mask, *parts, **options):
        return block_sum(left[mask], right, tiles[mask], *parts, **options)

    short, wide = jnp.bfloat16, jnp.float32
    first_two, last_two = partial_sum(2, (CUT, wide), (OWN - CUT, short))
    last_two_there = swap(last_two, 2)
    first, last = left[3]
    first, _ = lax.optimization_barrier((first, last_two))
    (first_three,) = block_sum([first], right, tiles[3], (CUT, short))
    handed = swap(first_three, 1)
    last, _ = lax.optimization_barrier((last, first_three))
    (last_three,) = block_sum([last], right, tiles[3], (OWN - CUT, short), at=CUT)
    arrived, firsts = [swap(last_three, 3)], [CUT]
    first_both = local(add_kernel, shape(first_two.shape, short), first_two, handed)
    arrived.append(swap(first_both, 2))
    firsts.append(0)
    left[1][0], _ = lax.optimization_barrier((left[1][0], last_three))
    for mask in [1, *range(4, col_count)]:
        arrived.append(swap(partial_sum(mask, (OWN, short))[0], mask))
        firsts.append(0)
    (own_sum,) = partial_sum(0, (OWN, wide), earlier=[last_two_there], flops=10**10)
    picked = local(
        functools.partial(select_kernel, per_owner, firsts),
        shape((LIST, NORB), jnp.bfloat16),
        wanted,
        own_sum,
        *arrived,
    )
    chosen = lax.all_to_all(
        picked.reshape(box_total, per_owner, NORB),
        ("row", "col"),
        split_axis=0,
        concat_axis=0,
        tiled=True,
    ).reshape(LIST, NORB)
    box, count = interp.shape[0], 4
    return pl.pallas_call(
        apply_kernel,
        out_shape=jax.ShapeDtypeStruct((box, NORB), jnp.float32),
        in_specs=[vmem(), vmem()],
        out_specs=hbm(),
        scratch_shapes=[
            pltpu.VMEM((count, box // count, NORB), jnp.float32),
            pltpu.SemaphoreType.DMA((count,)),
        ],
        compiler_params=params(),
    )(interp, chosen)


def solution(mesh):
    return jax.shard_map(
        shards,
        mesh=mesh,
        in_specs=(
            P(("row", "col"), None),
            P("row", "col"),
            P(("row", "col"), None),
            P(),
            P(),
            P(("row", "col"), None),
            P(("row", "col"), None),
        ),
        out_specs=P(("row", "col"), None),
        check_vma=False,
    )
```

```python
import functools

import jax
import jax.numpy as jnp
from jax import lax
from jax.experimental import pallas as pl
from jax.experimental.pallas import tpu as pltpu
from jax.sharding import PartitionSpec as P

NORB = 512
LIST = 1024
OWN = 256
SLOTS = 768
LANES = 128
CUT = 96
VMEM_LIMIT = 48 * 1024 * 1024
PICK_LIMIT = 60 * 1024 * 1024


def vmem():
    return pl.BlockSpec(memory_space=pltpu.VMEM)


def smem():
    return pl.BlockSpec(memory_space=pltpu.SMEM)


def hbm():
    return pl.BlockSpec(memory_space=pltpu.HBM)


def params(limit=VMEM_LIMIT):
    return pltpu.CompilerParams(vmem_limit_bytes=limit)


def pick_kernel(
    box_total, capacity, counts_hbm, grid_hbm, owner_hbm, listed_hbm, orbitals_hbm, result,
    counts, grid_rows, owner_map, listed, orbitals, out, sems, out_sems,
):
    copies = [
        pltpu.make_async_copy(source, target, sems.at[n])
        for n, (source, target) in enumerate(
            [
                (counts_hbm, counts),
                (grid_hbm, grid_rows),
                (owner_hbm, owner_map),
                (listed_hbm, listed),
                (orbitals_hbm, orbitals),
            ]
        )
    ]
    for copy in copies:
        copy.start()
    targets = box_total * capacity
    my_box = lax.axis_index("row") * lax.axis_size("col") + lax.axis_index("col")
    copies[0].wait()
    start = jnp.int32(0)
    for b in range(box_total):
        start = start + jnp.where(b < my_box, counts[b], 0)
    stop = start + counts[my_box]
    first = start // LANES
    shift = start - first * LANES
    blocks = SLOTS // LANES + 1
    top = owner_map.shape[0] - 1
    lane = lax.broadcasted_iota(jnp.int32, (1, LANES), 1)
    copies[1].wait()
    copies[2].wait()
    turned = pltpu.roll(grid_rows[...], shift, 1)
    lane8 = lax.broadcasted_iota(jnp.int32, turned.shape, 1)
    lined = jnp.where(lane8 < shift, pltpu.roll(turned, 1, 0), turned)
    before = (
        lax.broadcasted_iota(jnp.int32, (LANES, LANES), 0)
        < lax.broadcasted_iota(jnp.int32, (LANES, LANES), 1)
    ).astype(jnp.bfloat16)
    owner_ids = lax.broadcasted_iota(jnp.int32, (box_total, LANES), 0)
    target_ids = lax.broadcasted_iota(jnp.int32, (targets, LANES), 0)
    base = jnp.zeros((box_total, 1), jnp.float32)
    found = jnp.zeros((targets, LANES), jnp.int32)
    for i in range(blocks):
        k = (first + i) * LANES + lane
        position = owner_map[pl.ds(jnp.minimum(first + i, top), 1), :]
        live = (k >= start) & (k < stop)
        owner = jnp.where(live, position // OWN, -1)
        member = (owner_ids == owner).astype(jnp.float32)
        inner = jnp.dot(member.astype(jnp.bfloat16), before, preferred_element_type=jnp.float32)
        rank = jnp.sum(member * (inner + base), axis=0, keepdims=True).astype(jnp.int32)
        base = base + jnp.sum(member, axis=1, keepdims=True)
        target = jnp.where(live, owner * capacity + rank, -1)
        found = found + jnp.where(target_ids == target, lined[i : i + 1, :] + 1, 0)
    source = jnp.sum(found.astype(jnp.float32), axis=1, keepdims=True).astype(jnp.int32) - 1
    copies[3].wait()
    per_owner = LIST // box_total
    fold = LANES // per_owner
    spread = jnp.broadcast_to(listed[...][:, None, :], (LIST // LANES, fold, LANES))
    spread = spread.reshape(box_total, LANES)
    phase = lax.broadcasted_iota(jnp.int32, spread.shape, 0) % fold
    indices = spread
    for q in range(1, fold):
        indices = jnp.where(phase == q, pltpu.roll(spread, LANES - q * per_owner, 1), indices)
    indices = indices.astype(jnp.float32).astype(jnp.bfloat16)
    tail = out.shape[1] - capacity * (NORB // LANES)
    out[:, capacity * (NORB // LANES) :, :] = jnp.broadcast_to(
        indices[:, None, :], (box_total, tail, LANES)
    )
    box = orbitals.shape[0]
    step = targets // 4
    sent = []
    copies[4].wait()
    for t in range(0, targets, step):
        hot = source[t : t + step] == lax.broadcasted_iota(jnp.int32, (step, box), 1)
        rows = jnp.dot(
            hot.astype(jnp.float32).astype(jnp.bfloat16),
            orbitals[...],
            preferred_element_type=jnp.float32,
        )
        owners = step // capacity
        packed = jnp.concatenate(
            [
                rows[:, c : c + LANES].reshape(owners, capacity, LANES)
                for c in range(0, NORB, LANES)
            ],
            axis=1,
        )
        first_owner = t // capacity
        out[first_owner : first_owner + owners, : packed.shape[1], :] = packed.astype(jnp.bfloat16)
        part = slice(first_owner, first_owner + owners)
        sent.append(
            pltpu.make_async_copy(out.at[part], result.at[part], out_sems.at[t // step])
        )
        sent[-1].start()
    for copy in sent:
        copy.wait()


def place_kernel(capacity, index, received, out, wanted):
    boxes = received.shape[0]
    packed = received[:, : capacity * (NORB // LANES), :].astype(jnp.float32)
    rows = jnp.concatenate(
        [
            packed[:, c * capacity : (c + 1) * capacity, :].reshape(boxes * capacity, LANES)
            for c in range(NORB // LANES)
        ],
        axis=1,
    ).astype(jnp.bfloat16)
    hot = index[...] == lax.broadcasted_iota(jnp.int32, (index.shape[0], rows.shape[0]), 1)
    out[...] = jnp.dot(
        hot.astype(jnp.float32).astype(jnp.bfloat16), rows, preferred_element_type=jnp.float32
    ).astype(jnp.bfloat16)
    tail = received[:, capacity * (NORB // LANES) :, :].astype(jnp.float32)
    wanted[...] = tail[:, 0, :].astype(jnp.int32)


def join_kernel(*refs):
    out, at = refs[-1], 0
    for ref in refs[:-1]:
        out[at : at + ref.shape[0], :] = ref[...]
        at += ref.shape[0]


def hold_kernel(*refs):
    count = len(refs) // 2
    for source, target in zip(refs[:count], refs[count:]):
        target[...] = source[...]


def pair_block(left, right):
    return lax.dot_general(
        left, right, (((1,), (1,)), ((), ())), preferred_element_type=jnp.float32
    ).astype(jnp.bfloat16)


def order_kernel(masks, scalars, *refs):
    pieces, out = refs[:-1], refs[-1]
    places = [mask ^ parity for parity in (0, 1) for mask in masks]
    for ref in pieces:
        for n in range(ref.shape[0] // OWN):
            place = jnp.bitwise_xor(scalars[0], places.pop(0)) * OWN
            out[pl.ds(pl.multiple_of(place, OWN), OWN), :] = ref[n * OWN : (n + 1) * OWN, :]


def fetch_kernel(scalars, coulomb, *refs):
    outs, sems = refs[:-1], refs[-1]
    copies = []
    for n, out in enumerate(outs):
        source = pl.ds(pl.multiple_of(scalars[n] * OWN, OWN), OWN)
        copies.append(pltpu.make_async_copy(coulomb.at[source, :], out, sems.at[n]))
        copies[-1].start()
    for copy in copies:
        copy.wait()


def block_kernel(count, spans, at, *refs):
    lefts, right, tile = refs[:count], refs[count], refs[count + 1]
    earlier, outs, weighted = refs[count + 2 : -1 - len(spans)], refs[-1 - len(spans) : -1], refs[-1]
    left = jnp.concatenate([ref[...] for ref in lefts]) if count > 1 else lefts[0][...]
    rows = slice(at, at + left.shape[0])
    step = 512
    for t in range(0, right.shape[0], step):
        pair = pair_block(left, right[t : t + step, :]).astype(jnp.float32)
        weighted[:, t : t + step] = (
            pair * tile[rows, t : t + step].astype(jnp.float32)
        ).astype(jnp.bfloat16)
    total = jnp.dot(weighted[...], right[...], preferred_element_type=jnp.float32)
    for out, (low, high) in zip(outs, spans):
        out[...] = total[low:high, :].astype(out.dtype)
    for ref in earlier:
        low = total.shape[0] - ref.shape[0]
        outs[0][low:, :] = total[low:, :] + ref[...].astype(jnp.float32)


def add_kernel(one, other, out):
    out[...] = (one[...] + other[...].astype(jnp.float32)).astype(out.dtype)


def block_sum(lefts, right, tile, *parts, at=0, earlier=(), flops=0):
    spans, low = [], 0
    for rows, _ in parts:
        spans.append((low, low + rows))
        low += rows
    return local(
        functools.partial(block_kernel, len(lefts), spans, at),
        tuple(jax.ShapeDtypeStruct((rows, NORB), dtype) for rows, dtype in parts),
        *lefts,
        right,
        tile,
        *earlier,
        flops=flops,
        scratch=[pltpu.VMEM((low, right.shape[0]), jnp.bfloat16)],
    )


def local(kernel, out, *args, flops=0, far=None, scratch=()):
    def spec(n, a):
        if n == far:
            return hbm()
        return smem() if a.ndim == 1 else vmem()

    return pl.pallas_call(
        kernel,
        out_shape=out,
        in_specs=[spec(n, a) for n, a in enumerate(args)],
        out_specs=jax.tree.map(lambda _: vmem(), out),
        scratch_shapes=scratch,
        compiler_params=params(),
        cost_estimate=pl.CostEstimate(flops=flops, bytes_accessed=0, transcendentals=0),
    )(*args)


def select_kernel(per_owner, firsts, index, own, *refs):
    boxes = index.shape[0]
    spread = jnp.broadcast_to(index[...][:, None, :], (boxes, per_owner, LANES))
    diagonal = lax.broadcasted_iota(jnp.int32, spread.shape, 1) == lax.broadcasted_iota(
        jnp.int32, spread.shape, 2
    )
    picks = jnp.sum(jnp.where(diagonal, spread, 0).astype(jnp.float32), axis=2, keepdims=True)
    picks = picks.reshape(boxes * per_owner, 1).astype(jnp.int32)
    out = refs[-1]
    totals = []
    for low, high in ((0, CUT), (CUT, OWN)):
        total = own[low:high, :]
        for ref, first in zip(refs[:-1], firsts):
            if first <= low < first + ref.shape[0]:
                total = total + ref[low - first : high - first, :].astype(jnp.float32)
        totals.append(total.astype(jnp.bfloat16))
    projected = jnp.concatenate(totals)
    hot = picks == lax.broadcasted_iota(jnp.int32, (boxes * per_owner, OWN), 1)
    out[...] = jnp.dot(
        hot.astype(jnp.float32).astype(jnp.bfloat16), projected, preferred_element_type=jnp.float32
    ).astype(jnp.bfloat16)


def apply_kernel(interp, chosen, out, parts, sems):
    rows = parts.shape[1]
    copies = []
    for n in range(parts.shape[0]):
        parts[n] = -jnp.dot(
            interp[n * rows : (n + 1) * rows, :], chosen[...], preferred_element_type=jnp.float32
        )
        target = out.at[n * rows : (n + 1) * rows, :]
        copies.append(pltpu.make_async_copy(parts.at[n], target, sems.at[n]))
        copies[-1].start()
    for copy in copies:
        copy.wait()


def shards(orbitals, coulomb, interp, box_counts, owner_map, grid_rows, listed):
    row_count = lax.axis_size("row")
    col_count = lax.axis_size("col")
    box_total = row_count * col_count
    point_total = OWN * box_total
    capacity = (SLOTS + box_total - 1) // box_total
    per_owner = LIST // box_total
    my_row, my_col = lax.axis_index("row"), lax.axis_index("col")
    my_box = my_row * col_count + my_col
    packed = capacity * (NORB // LANES)
    packed = (packed // 8 + 1) * 8
    outgoing = pl.pallas_call(
        functools.partial(pick_kernel, box_total, capacity),
        out_shape=jax.ShapeDtypeStruct((box_total, packed, LANES), jnp.bfloat16),
        in_specs=[hbm()] * 5,
        out_specs=hbm(),
        scratch_shapes=[
            pltpu.SMEM((box_total,), jnp.int32),
            pltpu.VMEM((grid_rows.shape[1] // LANES, LANES), jnp.int32),
            pltpu.VMEM((point_total // LANES, LANES), jnp.int32),
            pltpu.VMEM((LIST // LANES, LANES), jnp.int32),
            pltpu.VMEM(orbitals.shape, jnp.bfloat16),
            pltpu.VMEM((box_total, packed, LANES), jnp.bfloat16),
            pltpu.SemaphoreType.DMA((5,)),
            pltpu.SemaphoreType.DMA((4,)),
        ],
        compiler_params=params(PICK_LIMIT),
        cost_estimate=pl.CostEstimate(
            flops=2 * SLOTS * LIST * NORB, bytes_accessed=2 << 20, transcendentals=0
        ),
    )(
        box_counts,
        grid_rows.reshape(grid_rows.shape[1] // LANES, LANES),
        owner_map.reshape(point_total // LANES, LANES),
        listed.reshape(LIST // LANES, LANES),
        orbitals,
    )
    received = lax.all_to_all(
        outgoing, ("row", "col"), split_axis=0, concat_axis=0, tiled=True
    )

    wanted_pos = my_box * OWN + jnp.arange(OWN, dtype=jnp.int32)
    all_listing = jnp.arange(point_total, dtype=jnp.int32)
    my_points = jnp.sum(
        jnp.where(owner_map[None, :] == wanted_pos[:, None], all_listing[None, :], 0), axis=1
    )
    box_ends = jnp.cumsum(box_counts)
    source = jnp.sum((my_points[:, None] >= box_ends[None, :]).astype(jnp.int32), axis=1)
    earlier = (source[:, None] == source[None, :]) & (my_points[None, :] < my_points[:, None])
    source_rank = jnp.sum(earlier.astype(jnp.int32), axis=1)
    index = (source * capacity + source_rank).reshape(OWN, 1)
    owned_rows, wanted = pl.pallas_call(
        functools.partial(place_kernel, capacity),
        out_shape=(
            jax.ShapeDtypeStruct((OWN, NORB), jnp.bfloat16),
            jax.ShapeDtypeStruct((box_total, LANES), jnp.int32),
        ),
        in_specs=[vmem(), vmem()],
        out_specs=(vmem(), vmem()),
        compiler_params=params(),
    )(index, received)

    def swap(rows, mask):
        return lax.ppermute(rows, "col", [(i, i ^ mask) for i in range(col_count)])

    def join(*rows):
        total = sum(r.shape[0] for r in rows)
        return local(join_kernel, jax.ShapeDtypeStruct((total, NORB), rows[0].dtype), *rows)

    def flip(rows, mask):
        return lax.ppermute(rows, "row", [(i, i ^ mask) for i in range(row_count)])

    half = OWN // 2
    left = {0: [owned_rows]}
    for mask in range(1, col_count):
        if mask & (mask - 1) == 0:
            left[mask] = [swap(owned_rows, mask)]

    whole = {0: owned_rows}
    single = [1 << b for b in range(1, row_count.bit_length() - 1)]
    double = [mask for mask in range(2, row_count, 2) if mask not in single]
    for mask in single:
        whole[mask] = flip(owned_rows, mask)
    tiles = local(
        fetch_kernel,
        tuple(jax.ShapeDtypeStruct((OWN, row_count * OWN), jnp.bfloat16) for _ in range(col_count)),
        jnp.bitwise_xor(my_col, jnp.arange(col_count)).astype(jnp.int32),
        coulomb,
        far=1,
        scratch=[pltpu.SemaphoreType.DMA((col_count,))],
    )

    whole[single[0]], *tiles = lax.optimization_barrier((whole[single[0]], *tiles))
    passed_on = [owned_rows, join(*[whole[mask] for mask in single])]
    for mask in double:
        low, high = mask & -mask, 1 << (mask.bit_length() - 1)
        whole[mask] = join(
            flip(whole[mask ^ high][:half], high), flip(whole[mask ^ low][half:], low)
        )
    if double:
        passed_on.append(join(*[whole[mask] for mask in double]))
    masks = [0] + single + double
    shape = jax.ShapeDtypeStruct
    mirrored = [flip(rows, 1) for rows in passed_on]
    direct = [mask for mask in left if mask]
    held = local(
        hold_kernel,
        tuple(shape(owned_rows.shape, owned_rows.dtype) for _ in direct),
        *[left[mask][0] for mask in direct],
        flops=20 * 10**9,
    )
    left.update((mask, [rows]) for mask, rows in zip(direct, held))
    for mask in range(3, col_count):
        if mask not in left:
            low = mask & -mask
            (rows,) = left[mask ^ low]
            parts = [rows[:CUT], rows[CUT:]] if mask == 3 else [rows]
            left[mask] = [swap(part, low) for part in parts]

    right = local(
        functools.partial(order_kernel, masks),
        shape((row_count * OWN, NORB), jnp.bfloat16),
        my_row.reshape(1).astype(jnp.int32),
        *passed_on,
        *mirrored,
    )
    def partial_sum(mask, *parts, **options):
        return block_sum(left[mask], right, tiles[mask], *parts, **options)

    short, wide = jnp.bfloat16, jnp.float32
    first_two, last_two = partial_sum(2, (CUT, wide), (OWN - CUT, short))
    last_two_there = swap(last_two, 2)
    first, last = left[3]
    first, _ = lax.optimization_barrier((first, last_two))
    (first_three,) = block_sum([first], right, tiles[3], (CUT, short))
    handed = swap(first_three, 1)
    (last_three,) = block_sum([last], right, tiles[3], (OWN - CUT, short), at=CUT)
    arrived, firsts = [swap(last_three, 3)], [CUT]
    first_both = local(add_kernel, shape(first_two.shape, short), first_two, handed)
    arrived.append(swap(first_both, 2))
    firsts.append(0)
    left[1][0], _ = lax.optimization_barrier((left[1][0], last_three))
    for mask in [1, *range(4, col_count)]:
        arrived.append(swap(partial_sum(mask, (OWN, short))[0], mask))
        firsts.append(0)
    (own_sum,) = partial_sum(0, (OWN, wide), earlier=[last_two_there], flops=10**10)
    picked = local(
        functools.partial(select_kernel, per_owner, firsts),
        shape((LIST, NORB), jnp.bfloat16),
        wanted,
        own_sum,
        *arrived,
    )
    chosen = lax.all_to_all(
        picked.reshape(box_total, per_owner, NORB),
        ("row", "col"),
        split_axis=0,
        concat_axis=0,
        tiled=True,
    ).reshape(LIST, NORB)
    box, count = interp.shape[0], 4
    return pl.pallas_call(
        apply_kernel,
        out_shape=jax.ShapeDtypeStruct((box, NORB), jnp.float32),
        in_specs=[vmem(), vmem()],
        out_specs=hbm(),
        scratch_shapes=[
            pltpu.VMEM((count, box // count, NORB), jnp.float32),
            pltpu.SemaphoreType.DMA((count,)),
        ],
        compiler_params=params(),
    )(interp, chosen)


def solution(mesh):
    return jax.shard_map(
        shards,
        mesh=mesh,
        in_specs=(
            P(("row", "col"), None),
            P("row", "col"),
            P(("row", "col"), None),
            P(),
            P(),
            P(("row", "col"), None),
            P(("row", "col"), None),
        ),
        out_specs=P(("row", "col"), None),
        check_vma=False,
    )
```
